32 devices in a mesh: hi: 4 (over y, x), lo: 8 (over z, core).
Axes of the slice: x: 2, y: 2, z: 4, core: 2. Of those that a mesh axis runs over, the one named last changes fastest.
Arguments:
- charges: bfloat16 [262144, 128], P(('hi', 'lo')), may hold values from -6 to 6
- source_order: int32 [262144], P(('hi', 'lo')), may hold values from 0 to 8191, as said below
- source_interp: bfloat16 [262144, 128], P(('hi', 'lo')), may hold values from -0.5 to 0.5
- factors: bfloat16 [4096, 8, 128], P(('hi', 'lo')), may hold values from -6 to 6
- transfers: bfloat16 [8, 2, 2, 64, 128], replicated, may hold values from -0.375 to 0.375
- level_bits: int32 [4], replicated, may hold values from 0 to 6
- receiver_interp: bfloat16 [262144, 128], P(('hi', 'lo')), may hold values from -0.5 to 0.5
- receiver_slot: int32 [262144], P(('hi', 'lo')), may hold values from 0 to 8191, as said below
Outputs:
- displacement: bfloat16 [262144, 128], P(('hi', 'lo'))
The draws below stay inside these ranges and needn't reach their ends.
Inputs may be any that keep to these rules, and one draw needn't show every extreme that they name: `source_order`: each aligned block of 8192 entries is a permutation of 0 to 8191. `receiver_slot`: each aligned block of 8192 entries is a permutation of 0 to 8191.
All inputs are finite; a program needn't handle non-finite values.
Results may differ from the reference program's by a relative error of at most 0.019.
Values may be sent and summed in bfloat16 or wider, within the bound.
No kernel may reach another device: no remote copies, remote signals or barrier semaphores. Data moves between devices by JAX's collectives and lax.ppermute only.
A program may use at most 64 MiB of HBM per device.

```python
import jax
import jax.numpy as jnp
from jax import lax

RANK = 64
RHS = 64
LEAF = 64
BLK_DEV = 128
BLOCKS = 4096
PTS_DEV = 8192
POINTS = 262144
N_LO = 8
DEVICES = 32


def block_permutations(key):
    keys = jax.random.split(key, POINTS // PTS_DEV)
    perms = jax.vmap(lambda single: jax.random.permutation(single, PTS_DEV))(keys)
    return perms.reshape(-1).astype(jnp.int32)


def draw_source_order(key, part):
    return block_permutations(jax.random.fold_in(key, 11))


def draw_receiver_slot(key, part):
    return block_permutations(jax.random.fold_in(key, 29))


def place_ends(array, own_key, least, largest):
    longest = array.shape.index(max(array.shape))
    spots = []
    for shift in (0, 1):
        where = [jax.random.randint(jax.random.fold_in(own_key, axis), (), 0, length) for axis, length in enumerate(array.shape)]
        where[longest] = (where[longest] + shift) % array.shape[longest]
        spots.append(tuple(where))
    return array.at[spots[0]].set(least).at[spots[1]].set(largest)


def steps_of(key, dims, shards, least, top_value):
    loudness = 1.0
    for dim, parts in shards:
        steps = jax.random.uniform(jax.random.fold_in(jax.random.fold_in(key, 6), dim), (parts,), jnp.float32, least / len(shards), top_value / len(shards))
        loudness = loudness * jnp.repeat(jnp.exp(steps), dims[dim] // parts).reshape((-1,) + (1,) * (len(dims) - 1 - dim))
    return loudness


def bell_draw(rng, dims, scale, reach, cuts=(), held_as=jnp.bfloat16):
    entries = scale * jax.random.normal(rng, dims, jnp.float32)
    if cuts:
        entries = entries * steps_of(rng, dims, cuts, -0.22, 0.18)
    return jnp.clip(entries, -reach, reach).astype(held_as)


def setup_inputs(seed: int = 0) -> dict:
    splits = jax.random.split(jax.random.key(seed), 9)
    return {
        "charges": bell_draw(splits[0], (POINTS, 2 * RHS), 0.7071, 6.0, ((0, 32),)),
        "source_order": draw_source_order(jax.random.fold_in(splits[8], 71), 0),
        "source_interp": bell_draw(splits[2], (POINTS, 2 * RANK), (2 * LEAF) ** -0.5, 0.5, ((0, 32),)),
        "factors": bell_draw(splits[3], (BLOCKS, 8, 2 * RANK), 0.7071, 6.0, ((0, 32),)),
        "transfers": bell_draw(splits[4], (8, 2, 2, RANK, 2 * RANK), (4 * RANK) ** -0.5, 0.375),
        "level_bits": place_ends(jax.random.randint(splits[5], (4,), 0, 7), jax.random.fold_in(splits[5], 1), 0, 6).astype(jnp.int32),
        "receiver_interp": bell_draw(splits[6], (POINTS, 2 * RANK), (2 * RANK) ** -0.5, 0.5, ((0, 32),)),
        "receiver_slot": draw_receiver_slot(jax.random.fold_in(splits[8], 71), 0),
    }


def real_form(block_piece):
    rank_size = block_piece.shape[0]
    real_part = block_piece[:, :rank_size]
    imag_part = block_piece[:, rank_size:]
    lower_rows = jnp.concatenate([-imag_part, real_part], axis=1)
    return jnp.concatenate([block_piece, lower_rows], axis=0)


def times_factor(values, factor):
    rank_size = factor.shape[-1] // 2
    widened = factor.astype(jnp.float32)[:, None, :]
    factor_re = widened[..., :rank_size]
    factor_im = widened[..., rank_size:]
    values_re = values[..., :rank_size]
    values_im = values[..., rank_size:]
    return jnp.concatenate([values_re * factor_re - values_im * factor_im, values_re * factor_im + values_im * factor_re], axis=-1)


def apply_matrix(coeffs, matrix):
    pair_width = coeffs.shape[-1]
    flattened = coeffs.reshape(-1, pair_width)
    return jnp.dot(flattened, real_form(matrix), preferred_element_type=jnp.float32).reshape(coeffs.shape)


def mix_halves(lower_half, upper_half, matrices):
    child_zero = apply_matrix(lower_half, matrices[0, 0]) + apply_matrix(upper_half, matrices[0, 1])
    child_one = apply_matrix(lower_half, matrices[1, 0]) + apply_matrix(upper_half, matrices[1, 1])
    return child_zero, child_one


def pair_level(coeffs, factor, matrices, stride):
    blocks_here = coeffs.shape[0]
    half_index = jnp.arange(blocks_here // 2, dtype=jnp.int32)
    lower_index = (half_index // stride) * (2 * stride) + half_index % stride
    upper_index = lower_index + stride
    child_zero, child_one = mix_halves(coeffs[lower_index], coeffs[upper_index], matrices)
    blocks = jnp.arange(blocks_here, dtype=jnp.int32)
    child_bit = (blocks // stride) % 2
    position = child_bit * (blocks_here // 2) + (blocks // (2 * stride)) * stride + blocks % stride
    merged = jnp.concatenate([child_zero, child_one], axis=0)[position]
    return times_factor(merged, factor).astype(jnp.bfloat16)


def leaf_coeffs(pair_rows):
    charge_rows, interp_rows = pair_rows
    rhs_count = charge_rows.shape[-1] // 2
    rank_size = interp_rows.shape[-1] // 2
    products = jnp.einsum("bmk,bmr->bkr", charge_rows.astype(jnp.float32), interp_rows.astype(jnp.float32))
    real_part = products[:, :rhs_count, :rank_size] - products[:, rhs_count:, rank_size:]
    imag_part = products[:, :rhs_count, rank_size:] + products[:, rhs_count:, :rank_size]
    return jnp.concatenate([real_part, imag_part], axis=-1).astype(jnp.bfloat16)


def receiver_values(pair_rows):
    interp_rows, final_rows = pair_rows
    rank_size = interp_rows.shape[-1] // 2
    coeff_re = final_rows[..., :rank_size]
    coeff_im = final_rows[..., rank_size:]
    stacked = jnp.concatenate([jnp.concatenate([coeff_re, -coeff_im], axis=-1), jnp.concatenate([coeff_im, coeff_re], axis=-1)], axis=1)
    values = jnp.einsum("bmr,bnr->bmn", interp_rows.astype(jnp.float32), stacked.astype(jnp.float32))
    return values.astype(jnp.bfloat16)


def reference(charges, source_order, source_interp, factors, transfers, level_bits, receiver_interp, receiver_slot):
    device_rows = (jnp.arange(POINTS, dtype=jnp.int32) // PTS_DEV) * PTS_DEV
    ordered = charges[device_rows + source_order]
    coeffs = lax.map(leaf_coeffs, (ordered.reshape(DEVICES, BLK_DEV, LEAF, 2 * RHS), source_interp.reshape(DEVICES, BLK_DEV, LEAF, 2 * RANK)))
    coeffs = coeffs.reshape(BLOCKS, RHS, 2 * RANK)
    strides = jnp.left_shift(jnp.int32(1), level_bits)
    coeffs = pair_level(coeffs, factors[:, 0], transfers[0], strides[0])
    coeffs = pair_level(coeffs, factors[:, 1], transfers[1], strides[1])
    coeffs = pair_level(coeffs, factors[:, 2], transfers[2], BLK_DEV * N_LO // 2)
    coeffs = pair_level(coeffs, factors[:, 3], transfers[3], BLOCKS // 2)
    share_size = BLK_DEV // DEVICES
    switched = coeffs.reshape(DEVICES, DEVICES, share_size, RHS, 2 * RANK).transpose(1, 0, 2, 3, 4).reshape(BLOCKS, RHS, 2 * RANK)
    moved_factors = factors[:, 4:].reshape(DEVICES, DEVICES, share_size, 4, 2 * RANK).transpose(1, 0, 2, 3, 4).reshape(BLOCKS, 4, 2 * RANK)
    coeffs = pair_level(switched, moved_factors[:, 0], transfers[4], strides[2])
    coeffs = pair_level(coeffs, moved_factors[:, 1], transfers[5], strides[3])
    coeffs = pair_level(coeffs, moved_factors[:, 2], transfers[6], BLK_DEV * N_LO // 2)
    coeffs = pair_level(coeffs, moved_factors[:, 3], transfers[7], BLOCKS // 2)
    tree_values = lax.map(receiver_values, (receiver_interp.reshape(DEVICES, BLK_DEV, LEAF, 2 * RANK), coeffs.reshape(DEVICES, BLK_DEV, RHS, 2 * RANK)))
    tree_values = tree_values.reshape(POINTS, 2 * RHS)
    return tree_values[device_rows + receiver_slot]
```

```python
import functools

import jax
import jax.numpy as jnp
from jax import lax
from jax.experimental import pallas as pl
from jax.experimental.pallas import tpu as pltpu
from jax.sharding import PartitionSpec as P

LEAF = 64
AXES = ("hi", "lo")
BATCH = 16
F32 = jnp.float32
BF16 = jnp.bfloat16


def log2(value):
    return value.bit_length() - 1


def lanes_low(shape):
    return lax.broadcasted_iota(jnp.int32, shape, len(shape) - 1) < 64


def roll64(value):
    return pltpu.roll(value, 64, 1)


def build_weights(w_ref, slot, tr_ref, level, flip=0):
    for i in range(2):
        for c in range(2):
            piece = tr_ref[level, c ^ flip, i ^ flip].astype(F32)
            turned = roll64(piece)
            turned = jnp.where(lanes_low(piece.shape), -turned, turned)
            block = jnp.concatenate([piece, turned], axis=0).astype(BF16)
            w_ref[slot, i * 128 : (i + 1) * 128, c * 128 : (c + 1) * 128] = block


def split_factors(read16, fa_ref, fb_ref, first, rows):
    def body(step, carry):
        for part in range(4):
            at = pl.multiple_of(step * 64 + part * 16, 16)
            fac = read16(at).astype(F32)
            turned = roll64(fac)
            low = lanes_low(fac.shape)
            fa_ref[pl.ds(first + at, 16), :] = jnp.where(low, fac, turned)
            fb_ref[pl.ds(first + at, 16), :] = jnp.where(low, -turned, fac)
        return carry

    lax.fori_loop(0, rows // 64, body, 0)


def scaled(value, fa_ref, fb_ref, row):
    fa = fa_ref[pl.ds(row, 1), :]
    fb = fb_ref[pl.ds(row, 1), :]
    return (value * fa + roll64(value) * fb).astype(BF16)


def gather16(rows_ref, index_ref, first):
    iota = lax.broadcasted_iota(jnp.int32, (8, 128), 0)
    halves = []
    for half in range(2):
        acc = None
        for i in range(8):
            at = index_ref[first + half * 8 + i]
            row = jnp.broadcast_to(rows_ref[pl.ds(at, 1), :], (8, 128))
            acc = row if acc is None else jnp.where(iota == i, row, acc)
        halves.append(acc)
    return jnp.concatenate(halves, axis=0).astype(BF16)


def pair_of(k, bit):
    low = k & (lax.shift_left(1, bit) - 1)
    first = lax.shift_left(lax.shift_right_logical(k, bit), bit + 1) | low
    return first, first + lax.shift_left(1, bit)


def source_kernel(dims, order_ref, bits_ref, ch_ref, si_ref, fac_ref, tr_ref, out_ref, x32, coef, fa, fb, w_ref):
    n_hi, n_lo, share, blocks, rhs = dims
    quarter = rhs // 4
    points = blocks * LEAF

    def widen(step, carry):
        rows = pl.ds(pl.multiple_of(step * 256, 256), 256)
        x32[rows, :] = ch_ref[rows, :].astype(F32)
        return carry

    lax.fori_loop(0, points // 256, widen, 0)
    build_weights(w_ref, 0, tr_ref, 0)
    build_weights(w_ref, 1, tr_ref, 1)
    split_factors(lambda at: fac_ref[pl.ds(at, 16), :], fa, fb, 0, blocks * 8)

    def leaf(step, carry):
        for part in range(2):
            b = step * 2 + part
            first = pl.multiple_of(b * LEAF, LEAF)
            rows = jnp.concatenate([gather16(x32, order_ref, first + g * 16) for g in range(LEAF // 16)], axis=0)
            product = lax.dot_general(
                rows, si_ref[pl.ds(first, LEAF), :], (((0,), (0,)), ((), ())), preferred_element_type=F32
            )
            lower = roll64(product[rhs:])
            lower = jnp.where(lanes_low(lower.shape), -lower, lower)
            coef[b] = (product[:rhs] + lower).astype(BF16)
        return carry

    lax.fori_loop(0, blocks // 2, leaf, 0)

    st, lm, hh = log2(share), log2(n_lo // 4), log2(n_hi // 2)

    def store_first(n, value):
        coef[n] = value

    def store_second(n, value):
        t = n & (share - 1)
        core = (n >> st) & 1
        mid = (n >> (st + 1)) & (n_lo // 4 - 1)
        z1 = (n >> (st + 1 + lm)) & 1
        rest = (n >> (st + 2 + lm)) & (n_hi // 2 - 1)
        y = n >> (st + 2 + lm + hh)
        target = rest * n_lo + core * (n_lo // 2) + mid * 2
        m = (y * 2 + z1) * share + t
        for r in range(4):
            d = target + (r // 2) * (n_hi // 2) * n_lo + r % 2
            out_ref[d * (4 * share) + m] = value[r * quarter : (r + 1) * quarter]

    def level(index, store):
        bit = bits_ref[index]

        def body(step, carry):
            ends = [pair_of(step * 4 + p, bit) for p in range(4)]
            lhs = jnp.concatenate([jnp.concatenate([coef[a], coef[b]], axis=1) for a, b in ends], axis=0)
            res = jnp.dot(lhs, w_ref[index], preferred_element_type=F32)
            for p in range(4):
                for c in range(2):
                    n = ends[p][c]
                    value = res[p * rhs : (p + 1) * rhs, c * 128 : (c + 1) * 128]
                    store(n, scaled(value, fa, fb, n * 8 + index))
            return carry

        lax.fori_loop(0, blocks // 8, body, 0)

    level(0, store_first)
    level(1, store_second)


def middle_kernel(dims, me_ref, bits_ref, g_ref, f0, f1, f2, f3, tr_ref, o0, o1, o2, o3, x, fa, fb, w_ref):
    n_hi, n_lo, share, blocks, rhs = dims
    quarter = rhs // 4
    st = log2(share)
    y, core = me_ref[0], me_ref[1]
    for index in range(4):
        build_weights(w_ref, index, tr_ref, index + 2)
    build_weights(w_ref, 4, tr_ref, 6, core)
    build_weights(w_ref, 5, tr_ref, 7, y)
    for j, f_ref in enumerate((f0, f1, f2, f3)):
        split_factors(lambda at, f_ref=f_ref: f_ref[pl.ds(at, 16), :], fa, fb, j * blocks * 8, blocks * 8)

    rounds = blocks // 2 // BATCH

    def read_arrived(j, n):
        first = (((j >> 1) ^ y) * 2 + ((j & 1) ^ core)) * share
        return g_ref[(n >> st) * (4 * share) + first + (n & (share - 1))]

    def read_held(j, n):
        return x[j * blocks + n]

    def level(index, bit, read):
        def body(step, carry):
            j = step // rounds
            ends = [pair_of((step % rounds) * BATCH + p, bit) for p in range(BATCH)]
            lhs = jnp.concatenate([jnp.concatenate([read(j, a), read(j, b)], axis=1) for a, b in ends], axis=0)
            res = jnp.dot(lhs, w_ref[index - 2], preferred_element_type=F32)
            for p in range(BATCH):
                for c in range(2):
                    n = j * blocks + ends[p][c]
                    value = res[p * quarter : (p + 1) * quarter, c * 128 : (c + 1) * 128]
                    x[n] = scaled(value, fa, fb, n * 8 + index)
            return carry

        lax.fori_loop(0, 4 * rounds, body, 0)

    level(2, st + log2(n_lo) - 1, read_arrived)
    level(3, st + log2(n_lo) + log2(n_hi) - 1, read_held)
    level(4, bits_ref[2], read_held)
    level(5, bits_ref[3], read_held)

    def across(index, pairs, stores):
        for (a, b), store in zip(pairs, stores):

            def body(step, carry, a=a, b=b, store=store):
                first = pl.multiple_of(step * BATCH, BATCH)
                lhs = jnp.concatenate(
                    [x[pl.ds(j * blocks + first, BATCH)].reshape(BATCH * quarter, 128) for j in (a, b)], axis=1
                )
                res = jnp.dot(lhs, w_ref[index - 2], preferred_element_type=F32)
                for p in range(BATCH):
                    for c, j in enumerate((a, b)):
                        value = res[p * quarter : (p + 1) * quarter, c * 128 : (c + 1) * 128]
                        store[c](first + p, scaled(value, fa, fb, (j * blocks + first + p) * 8 + index))
                return carry

            lax.fori_loop(0, blocks // BATCH, body, 0)

    def hold(j):
        def store(n, value):
            x[j * blocks + n] = value

        return store

    def give(o_ref):
        def store(n, value):
            o_ref[n] = value

        return store

    across(6, ((0, 1), (2, 3)), ((hold(0), hold(1)), (hold(2), hold(3))))
    across(7, ((0, 2), (1, 3)), ((give(o0), give(o2)), (give(o1), give(o3))))


def receiver_kernel(dims, me_ref, slot_ref, ri_ref, p0, p1, p2, p3, out_ref, t32, stack):
    n_hi, n_lo, share, blocks, rhs = dims
    quarter = rhs // 4
    y, z1 = me_ref[0], me_ref[2]

    def values(step, carry):
        for part in range(2):
            b = step * 2 + part
            for j, p_ref in enumerate((p0, p1, p2, p3)):
                group = ((j >> 1) ^ y) * 2 + ((j & 1) ^ z1)
                at = pl.multiple_of(group * quarter, quarter)
                piece = p_ref[b].astype(F32)
                upper = jnp.where(lanes_low(piece.shape), piece, -piece)
                stack[part, pl.ds(at, quarter), :] = upper.astype(BF16)
                stack[part, pl.ds(at + rhs, quarter), :] = roll64(piece).astype(BF16)
            rows = pl.ds(pl.multiple_of(b * LEAF, LEAF), LEAF)
            t32[rows, :] = lax.dot_general(
                ri_ref[rows, :], stack[part], (((1,), (1,)), ((), ())), preferred_element_type=F32
            )
        return carry

    lax.fori_loop(0, blocks // 2, values, 0)

    def pick(step, carry):
        for g in range(4):
            first = pl.multiple_of(step * 64 + g * 16, 16)
            out_ref[pl.ds(first, 16), :] = gather16(t32, slot_ref, first)
        return carry

    lax.fori_loop(0, blocks * LEAF // 64, pick, 0)


def on_vmem():
    return pl.BlockSpec(memory_space=pltpu.VMEM)


def on_smem():
    return pl.BlockSpec(memory_space=pltpu.SMEM)


def params():
    return pltpu.CompilerParams(vmem_limit_bytes=48 * 2**20)


def per_device(
    n_hi, n_lo, charges, source_order, source_interp, factors, transfers, level_bits, receiver_interp, receiver_slot
):
    points, twice_rhs = charges.shape
    rhs = twice_rhs // 2
    blocks = points // LEAF
    devices = n_hi * n_lo
    share = blocks // devices
    quarter = rhs // 4
    dims = (n_hi, n_lo, share, blocks, rhs)
    half_hi, half_lo = n_hi // 2 * n_lo, n_lo // 2
    hi, lo = lax.axis_index("hi"), lax.axis_index("lo")
    me = jnp.stack([hi >> (log2(n_hi) - 1), lo & 1, lo >> (log2(n_lo) - 1)]).astype(jnp.int32)

    def swapped(device, j):
        flipped = device ^ (half_hi if j >> 1 else 0)
        core, top = flipped & 1, (flipped // half_lo) & 1
        base = flipped - core - top * half_lo
        return base + (core ^ (j & 1)) * half_lo + top

    spread = factors.reshape(n_hi, 2, n_lo // 4, 2, share, 8, 128).transpose(0, 3, 2, 1, 4, 5, 6)
    spread = lax.all_to_all(spread.reshape(blocks, 8, 128), AXES, split_axis=0, concat_axis=0, tiled=True)
    spread = spread.reshape(blocks * 8, 128)
    facs = [spread]
    for j in range(1, 4):
        mask = (half_hi if j >> 1 else 0) ^ (j & 1)
        facs.append(lax.ppermute(spread, AXES, [(s, s ^ mask) for s in range(devices)]))

    sent = pl.pallas_call(
        functools.partial(source_kernel, dims),
        out_shape=jax.ShapeDtypeStruct((devices * 4 * share, quarter, 128), BF16),
        in_specs=[on_smem(), on_smem(), on_vmem(), on_vmem(), on_vmem(), on_vmem()],
        out_specs=on_vmem(),
        scratch_shapes=[
            pltpu.VMEM((points, 128), F32),
            pltpu.VMEM((blocks, rhs, 128), BF16),
            pltpu.VMEM((blocks * 8, 128), F32),
            pltpu.VMEM((blocks * 8, 128), F32),
            pltpu.VMEM((2, 256, 256), BF16),
        ],
        compiler_params=params(),
        name="source_side",
    )(source_order, level_bits, charges, source_interp, factors.reshape(blocks * 8, 128), transfers)

    arrived = lax.all_to_all(sent, AXES, split_axis=0, concat_axis=0, tiled=True)

    piece = jax.ShapeDtypeStruct((blocks, quarter, 128), BF16)
    pieces = pl.pallas_call(
        functools.partial(middle_kernel, dims),
        out_shape=[piece] * 4,
        in_specs=[on_smem(), on_smem()] + [on_vmem()] * 6,
        out_specs=[on_vmem()] * 4,
        scratch_shapes=[
            pltpu.VMEM((4 * blocks, quarter, 128), BF16),
            pltpu.VMEM((4 * blocks * 8, 128), F32),
            pltpu.VMEM((4 * blocks * 8, 128), F32),
            pltpu.VMEM((6, 256, 256), BF16),
        ],
        compiler_params=params(),
        name="middle_levels",
    )(me, level_bits, arrived, *facs, transfers)

    homes = [
        lax.ppermute(pieces[j], AXES, [(s, swapped(s, j)) for s in range(devices)]) for j in range(4)
    ]

    return pl.pallas_call(
        functools.partial(receiver_kernel, dims),
        out_shape=jax.ShapeDtypeStruct((points, twice_rhs), BF16),
        in_specs=[on_smem(), on_smem()] + [on_vmem()] * 5,
        out_specs=on_vmem(),
        scratch_shapes=[pltpu.VMEM((points, 128), F32), pltpu.VMEM((2, 2 * rhs, 128), BF16)],
        compiler_params=params(),
        name="receiver_side",
    )(me, receiver_slot, receiver_interp, *homes)


def solution(mesh):
    body = functools.partial(per_device, mesh.shape["hi"], mesh.shape["lo"])
    return jax.shard_map(
        body,
        mesh=mesh,
        in_specs=(
            P(AXES, None),
            P(AXES),
            P(AXES, None),
            P(AXES, None, None),
            P(),
            P(),
            P(AXES, None),
            P(AXES),
        ),
        out_specs=P(AXES, None),
        check_vma=False,
    )
```

```python
import functools

import jax
import jax.numpy as jnp
from jax import lax
from jax.experimental import pallas as pl
from jax.experimental.pallas import tpu as pltpu
from jax.sharding import PartitionSpec as P

LEAF = 64
AXES = ("hi", "lo")
SPLIT = 16
STACKS = 16
LEAVES = 16
SPAIRS = 32
F32 = jnp.float32
BF16 = jnp.bfloat16


def log2(value):
    return value.bit_length() - 1


def lanes_low(shape):
    return lax.broadcasted_iota(jnp.int32, shape, len(shape) - 1) < 64


def roll64(value):
    return pltpu.roll(value, 64, 1)


def build_weights(w_ref, slot, tr_ref, level, flip=0):
    for i in range(2):
        for c in range(2):
            piece = tr_ref[level, c ^ flip, i ^ flip].astype(F32)
            turned = roll64(piece)
            turned = jnp.where(lanes_low(piece.shape), -turned, turned)
            block = jnp.concatenate([piece, turned], axis=0).astype(BF16)
            w_ref[slot, i * 128 : (i + 1) * 128, c * 128 : (c + 1) * 128] = block
            across = roll64(jnp.concatenate([piece, turned], axis=0)).astype(BF16)
            w_ref[slot, i * 128 : (i + 1) * 128, 256 + c * 128 : 256 + (c + 1) * 128] = across


def split_factors(read16, fa_ref, fb_ref, first, rows):
    def body(step, carry):
        for part in range(SPLIT):
            at = pl.multiple_of(step * (16 * SPLIT) + part * 16, 16)
            fac = read16(at).astype(F32)
            turned = roll64(fac)
            low = lanes_low(fac.shape)
            fa_ref[pl.ds(first + at, 16), :] = jnp.where(low, fac, turned)
            fb_ref[pl.ds(first + at, 16), :] = jnp.where(low, -turned, fac)
        return carry

    lax.fori_loop(0, rows // (16 * SPLIT), body, 0)


def scaled(value, other, fa_ref, fb_ref, row):
    fa = fa_ref[pl.ds(row, 1), :]
    fb = fb_ref[pl.ds(row, 1), :]
    return (value * fa + other * fb).astype(BF16)


def gather16(rows_ref, index_ref, first):
    iota = lax.broadcasted_iota(jnp.int32, (8, 128), 0)
    halves = []
    for half in range(2):
        acc = None
        for i in range(8):
            at = index_ref[first + half * 8 + i]
            row = jnp.broadcast_to(rows_ref[pl.ds(at, 1), :], (8, 128))
            acc = row if acc is None else jnp.where(iota == i, row, acc)
        halves.append(acc)
    return jnp.concatenate(halves, axis=0).astype(BF16)


def pair_of(k, bit):
    low = k & (lax.shift_left(1, bit) - 1)
    first = lax.shift_left(lax.shift_right_logical(k, bit), bit + 1) | low
    return first, first + lax.shift_left(1, bit)


def source_kernel(
    dims, order_ref, bits_ref, ch_hbm, si_hbm, fac_hbm, tr_hbm, out_ref,
    ch_ref, si_ref, fac_ref, tr_ref, sems, x32, coef, mid_ref, fa, fb, w_ref,
):
    n_hi, n_lo, share, blocks, rhs = dims
    quarter = rhs // 4
    points = blocks * LEAF
    part = points // 4
    copies = [
        pltpu.make_async_copy(ch_hbm.at[pl.ds(i * part, part)], ch_ref.at[pl.ds(i * part, part)], sems.at[i])
        for i in range(4)
    ]
    copies.append(pltpu.make_async_copy(fac_hbm, fac_ref, sems.at[4]))
    copies.append(pltpu.make_async_copy(tr_hbm.at[pl.ds(0, 2)], tr_ref, sems.at[5]))
    copies.append(pltpu.make_async_copy(si_hbm, si_ref, sems.at[6]))
    for copy in copies:
        copy.start()

    def widen(step, carry):
        rows = pl.ds(pl.multiple_of(step * 512, 512), 512)
        x32[rows, :] = ch_ref[rows, :].astype(F32)
        return carry

    for i in range(4):
        copies[i].wait()
        lax.fori_loop(i * (part // 512), (i + 1) * (part // 512), widen, 0)
    for copy in copies[4:]:
        copy.wait()
    build_weights(w_ref, 0, tr_ref, 0)
    build_weights(w_ref, 1, tr_ref, 1)
    split_factors(lambda at: fac_ref[pl.ds(at, 16), :], fa, fb, 0, blocks * 8)

    def leaf(step, carry):
        for part in range(LEAVES):
            b = step * LEAVES + part
            first = pl.multiple_of(b * LEAF, LEAF)
            rows = jnp.concatenate([gather16(x32, order_ref, first + g * 16) for g in range(LEAF // 16)], axis=0)
            product = lax.dot_general(
                rows, si_ref[pl.ds(first, LEAF), :], (((0,), (0,)), ((), ())), preferred_element_type=F32
            )
            lower = roll64(product[rhs:])
            lower = jnp.where(lanes_low(lower.shape), -lower, lower)
            coef[b] = (product[:rhs] + lower).astype(BF16)
        return carry

    lax.fori_loop(0, blocks // LEAVES, leaf, 0)

    st, lm, hh = log2(share), log2(n_lo // 4), log2(n_hi // 2)

    def store_first(n, value):
        mid_ref[n] = value

    def store_second(n, value):
        t = n & (share - 1)
        core = (n >> st) & 1
        lmid = (n >> (st + 1)) & (n_lo // 4 - 1)
        z1 = (n >> (st + 1 + lm)) & 1
        rest = (n >> (st + 2 + lm)) & (n_hi // 2 - 1)
        y = n >> (st + 2 + lm + hh)
        target = rest * n_lo + core * (n_lo // 2) + lmid * 2
        m = (y * 2 + z1) * share + t
        for r in range(4):
            d = target + (r // 2) * (n_hi // 2) * n_lo + r % 2
            out_ref[d * (4 * share) + m] = value[r * quarter : (r + 1) * quarter]

    def level(index, src, store):
        bit = bits_ref[index]

        def body(step, carry):
            ends = [pair_of(step * SPAIRS + p, bit) for p in range(SPAIRS)]
            lhs = jnp.concatenate([jnp.concatenate([src[a], src[b]], axis=1) for a, b in ends], axis=0)
            res = jnp.dot(lhs, w_ref[index], preferred_element_type=F32)
            for p in range(SPAIRS):
                for c in range(2):
                    n = ends[p][c]
                    value = res[p * rhs : (p + 1) * rhs, c * 128 : (c + 1) * 128]
                    other = res[p * rhs : (p + 1) * rhs, 256 + c * 128 : 256 + (c + 1) * 128]
                    store(n, scaled(value, other, fa, fb, n * 8 + index))
            return carry

        lax.fori_loop(0, blocks // 2 // SPAIRS, body, 0)

    level(0, coef, store_first)
    level(1, mid_ref, store_second)


def spare_bit(bits_ref, dims):
    n_hi, n_lo, share, blocks, rhs = dims
    inner = log2(share) + log2(n_lo) - 1
    outer = log2(share) + log2(n_lo) + log2(n_hi) - 1
    free = [bit for bit in range(outer) if bit != inner][:3]
    spare = jnp.int32(free[2])
    for bit in (free[1], free[0]):
        taken = (bits_ref[2] == bit) | (bits_ref[3] == bit)
        spare = jnp.where(taken, spare, bit)
    return spare, inner, outer


def with_bit(i, bit, value):
    low = i & (lax.shift_left(1, bit) - 1)
    return lax.shift_left(lax.shift_right_logical(i, bit), bit + 1) | low | (value << bit)


def prepare_kernel(dims, me_ref, f0, f1, f2, f3, tr_ref, fa, fb, w_ref):
    blocks = dims[3]
    for j, f_ref in enumerate((f0, f1, f2, f3)):
        split_factors(lambda at, f_ref=f_ref: f_ref[pl.ds(at, 16), :], fa, fb, j * blocks * 8, blocks * 8)
    for index in range(4):
        build_weights(w_ref, index, tr_ref, index + 2)
    build_weights(w_ref, 4, tr_ref, 6, me_ref[1])
    build_weights(w_ref, 5, tr_ref, 7, me_ref[0])


def middle_kernel(dims, half, me_ref, bits_ref, g_ref, fa, fb, w_ref, o0, o1, o2, o3, x, x2):
    n_hi, n_lo, share, blocks, rhs = dims
    quarter = rhs // 4
    st = log2(share)
    y, core = me_ref[0], me_ref[1]
    spare, inner, outer = spare_bit(bits_ref, dims)
    count = blocks // 2

    def read_arrived(j, i):
        n = with_bit(i, spare, half)
        first = (((j >> 1) ^ y) * 2 + ((j & 1) ^ core)) * share
        return g_ref[(n >> st) * (4 * share) + first + (n & (share - 1))]

    def held(x):
        def read(j, i):
            return x[j * count + i]

        return read

    def finish(res, p, c, row):
        value = res[p * quarter : (p + 1) * quarter, c * 128 : (c + 1) * 128]
        other = res[p * quarter : (p + 1) * quarter, 256 + c * 128 : 256 + (c + 1) * 128]
        return scaled(value, other, fa, fb, row)

    def level(index, bit, read, x):
        packed = bit - (bit > spare).astype(jnp.int32)
        ends = [pair_of(k, packed) for k in range(count // 2)]
        homes = [tuple(with_bit(i, spare, half) * 8 + index for i in pair) for pair in ends]
        for j in range(4):
            lhs = jnp.concatenate([jnp.concatenate([read(j, a), read(j, b)], axis=1) for a, b in ends], axis=0)
            res = jnp.dot(lhs, w_ref[index - 2], preferred_element_type=F32)
            for p in range(count // 2):
                for c in range(2):
                    x[j * count + ends[p][c]] = finish(res, p, c, j * blocks * 8 + homes[p][c])

    level(2, inner, read_arrived, x)
    level(3, outer, held(x), x2)
    level(4, bits_ref[2], held(x2), x)
    level(5, bits_ref[3], held(x), x2)

    homes = [with_bit(i, spare, half) * 8 for i in range(count)]

    def across(index, x, pairs, outs):
        for (a, b), (out_a, out_b) in zip(pairs, outs):
            lhs = jnp.concatenate(
                [x[pl.ds(j * count, count)].reshape(count * quarter, 128) for j in (a, b)], axis=1
            )
            res = jnp.dot(lhs, w_ref[index - 2], preferred_element_type=F32)
            for p in range(count):
                for c, (j, out) in enumerate(((a, out_a), (b, out_b))):
                    out[p] = finish(res, p, c, j * blocks * 8 + homes[p] + index)

    rest = [x.at[pl.ds(j * count, count)] for j in range(4)]
    across(6, x2, ((0, 1), (2, 3)), ((rest[0], rest[1]), (rest[2], rest[3])))
    across(7, x, ((0, 2), (1, 3)), ((o0, o2), (o1, o3)))


def receiver_values(dims, half, me_ref, bits_ref, ri_ref, pieces, stack, store):
    n_hi, n_lo, share, blocks, rhs = dims
    quarter = rhs // 4
    y, z1 = me_ref[0], me_ref[2]
    spare, _, _ = spare_bit(bits_ref, dims)

    def values(step, carry):
        for part in range(STACKS):
            i = step * STACKS + part
            for j, p_ref in enumerate(pieces):
                group = ((j >> 1) ^ y) * 2 + ((j & 1) ^ z1)
                at = pl.multiple_of(group * quarter, quarter)
                piece = p_ref[i].astype(F32)
                upper = jnp.where(lanes_low(piece.shape), piece, -piece)
                stack[part, pl.ds(at, quarter), :] = upper.astype(BF16)
                stack[part, pl.ds(at + rhs, quarter), :] = roll64(piece).astype(BF16)
            rows = pl.ds(pl.multiple_of(with_bit(i, spare, half) * LEAF, LEAF), LEAF)
            result = lax.dot_general(
                ri_ref[rows, :], stack[part], (((1,), (1,)), ((), ())), preferred_element_type=F32
            )
            store(pl.multiple_of(i * LEAF, LEAF), result)
        return carry

    lax.fori_loop(0, blocks // 2 // STACKS, values, 0)


def first_receivers(dims, me_ref, bits_ref, ri_ref, p0, p1, p2, p3, out_ref, stack):
    def store(at, result):
        out_ref[pl.ds(at, LEAF), :] = result.astype(BF16)

    receiver_values(dims, 0, me_ref, bits_ref, ri_ref, (p0, p1, p2, p3), stack, store)


def last_receivers(dims, me_ref, bits_ref, slot_ref, ri_ref, p0, p1, p2, p3, done_ref, out_ref, t32, stack):
    blocks = dims[3]
    points = blocks * LEAF

    def store(at, result):
        t32[pl.ds(points // 2 + at, LEAF), :] = result

    def widen(step, carry):
        rows = pl.ds(pl.multiple_of(step * 512, 512), 512)
        t32[rows, :] = done_ref[rows, :].astype(F32)
        return carry

    lax.fori_loop(0, points // 2 // 512, widen, 0)
    receiver_values(dims, 1, me_ref, bits_ref, ri_ref, (p0, p1, p2, p3), stack, store)

    def pick(step, carry):
        for g in range(4):
            first = pl.multiple_of(step * 64 + g * 16, 16)
            out_ref[pl.ds(first, 16), :] = gather16(t32, slot_ref, first)
        return carry

    lax.fori_loop(0, points // 64, pick, 0)


def on_vmem():
    return pl.BlockSpec(memory_space=pltpu.VMEM)


def on_any():
    return pl.BlockSpec(memory_space=pl.ANY)


def on_smem():
    return pl.BlockSpec(memory_space=pltpu.SMEM)


def params():
    return pltpu.CompilerParams(vmem_limit_bytes=48 * 2**20)


def per_device(
    n_hi, n_lo, charges, source_order, source_interp, factors, transfers, level_bits, receiver_interp, receiver_slot
):
    points, twice_rhs = charges.shape
    rhs = twice_rhs // 2
    blocks = points // LEAF
    devices = n_hi * n_lo
    share = blocks // devices
    quarter = rhs // 4
    dims = (n_hi, n_lo, share, blocks, rhs)
    half_hi, half_lo = n_hi // 2 * n_lo, n_lo // 2
    hi, lo = lax.axis_index("hi"), lax.axis_index("lo")
    me = jnp.stack([hi >> (log2(n_hi) - 1), lo & 1, lo >> (log2(n_lo) - 1)]).astype(jnp.int32)

    def swapped(device, j):
        flipped = device ^ (half_hi if j >> 1 else 0)
        core, top = flipped & 1, (flipped // half_lo) & 1
        base = flipped - core - top * half_lo
        return base + (core ^ (j & 1)) * half_lo + top

    spread = factors.reshape(n_hi, 2, n_lo // 4, 2, share, 8, 128).transpose(0, 3, 2, 1, 4, 5, 6)
    spread = lax.all_to_all(spread.reshape(blocks, 8, 128), AXES, split_axis=0, concat_axis=0, tiled=True)
    spread = spread.reshape(blocks * 8, 128)
    facs = [spread]
    for j in range(1, 4):
        mask = (half_hi if j >> 1 else 0) ^ (j & 1)
        facs.append(lax.ppermute(spread, AXES, [(s, s ^ mask) for s in range(devices)]))

    sent = pl.pallas_call(
        functools.partial(source_kernel, dims),
        out_shape=jax.ShapeDtypeStruct((devices * 4 * share, quarter, 128), BF16),
        in_specs=[on_smem(), on_smem()] + [on_any()] * 4,
        out_specs=on_vmem(),
        scratch_shapes=[
            pltpu.VMEM((points, 128), BF16),
            pltpu.VMEM((points, 128), BF16),
            pltpu.VMEM((blocks * 8, 128), BF16),
            pltpu.VMEM((2,) + transfers.shape[1:], BF16),
            pltpu.SemaphoreType.DMA((7,)),
            pltpu.VMEM((points, 128), F32),
            pltpu.VMEM((blocks, rhs, 128), BF16),
            pltpu.VMEM((blocks, rhs, 128), BF16),
            pltpu.VMEM((blocks * 8, 128), F32),
            pltpu.VMEM((blocks * 8, 128), F32),
            pltpu.VMEM((2, 256, 512), BF16),
        ],
        compiler_params=params(),
        name="source_side",
    )(source_order, level_bits, charges, source_interp, factors.reshape(blocks * 8, 128), transfers)

    arrived = lax.all_to_all(sent, AXES, split_axis=0, concat_axis=0, tiled=True)

    prepared = pl.pallas_call(
        functools.partial(prepare_kernel, dims),
        out_shape=[
            jax.ShapeDtypeStruct((4 * blocks * 8, 128), F32),
            jax.ShapeDtypeStruct((4 * blocks * 8, 128), F32),
            jax.ShapeDtypeStruct((6, 256, 512), BF16),
        ],
        in_specs=[on_smem()] + [on_vmem()] * 5,
        out_specs=[on_vmem()] * 3,
        compiler_params=params(),
        name="factors_and_weights",
    )(me, *facs, transfers)

    piece = jax.ShapeDtypeStruct((blocks // 2, quarter, 128), BF16)
    homes = []
    for half in range(2):
        pieces = pl.pallas_call(
            functools.partial(middle_kernel, dims, half),
            out_shape=[piece] * 4,
            in_specs=[on_smem(), on_smem()] + [on_vmem()] * 4,
            out_specs=[on_vmem()] * 4,
            scratch_shapes=[
                pltpu.VMEM((2 * blocks, quarter, 128), BF16),
                pltpu.VMEM((2 * blocks, quarter, 128), BF16),
            ],
            compiler_params=params(),
            name="middle_levels",
        )(me, level_bits, arrived, *prepared)
        homes.append(
            [lax.ppermute(pieces[j], AXES, [(s, swapped(s, j)) for s in range(devices)]) for j in range(4)]
        )

    spare, _, _ = spare_bit(level_bits, dims)
    leaf_of = receiver_slot // LEAF
    low = leaf_of & (lax.shift_left(1, spare) - 1)
    packed = ((leaf_of >> (spare + 1)) << spare) | low
    half_of = (leaf_of >> spare) & 1
    slots = half_of * (points // 2) + packed * LEAF + receiver_slot % LEAF

    done = pl.pallas_call(
        functools.partial(first_receivers, dims),
        out_shape=jax.ShapeDtypeStruct((points // 2, twice_rhs), BF16),
        in_specs=[on_smem(), on_smem()] + [on_vmem()] * 5,
        out_specs=on_vmem(),
        scratch_shapes=[pltpu.VMEM((STACKS, 2 * rhs, 128), BF16)],
        compiler_params=params(),
        name="first_receivers",
    )(me, level_bits, receiver_interp, *homes[0])
    return pl.pallas_call(
        functools.partial(last_receivers, dims),
        out_shape=jax.ShapeDtypeStruct((points, twice_rhs), BF16),
        in_specs=[on_smem(), on_smem(), on_smem()] + [on_vmem()] * 6,
        out_specs=on_vmem(),
        scratch_shapes=[pltpu.VMEM((points, 128), F32), pltpu.VMEM((STACKS, 2 * rhs, 128), BF16)],
        compiler_params=params(),
        name="last_receivers",
    )(me, level_bits, slots, receiver_interp, *homes[1], done)


def solution(mesh):
    body = functools.partial(per_device, mesh.shape["hi"], mesh.shape["lo"])
    return jax.shard_map(
        body,
        mesh=mesh,
        in_specs=(
            P(AXES, None),
            P(AXES),
            P(AXES, None),
            P(AXES, None, None),
            P(),
            P(),
            P(AXES, None),
            P(AXES),
        ),
        out_specs=P(AXES, None),
        check_vma=False,
    )
```

```python
import functools

import jax
import jax.numpy as jnp
from jax import lax
from jax.experimental import pallas as pl
from jax.experimental.pallas import tpu as pltpu
from jax.sharding import PartitionSpec as P

LEAF = 64
AXES = ("hi", "lo")
SPLIT = 16
STACKS = 16
LEAVES = 16
SPAIRS = 32
F32 = jnp.float32
BF16 = jnp.bfloat16


def log2(value):
    return value.bit_length() - 1


def lanes_low(shape):
    return lax.broadcasted_iota(jnp.int32, shape, len(shape) - 1) < 64


def roll64(value):
    return pltpu.roll(value, 64, 1)


def build_weights(w_ref, slot, tr_ref, level, flip=0):
    for i in range(2):
        for c in range(2):
            piece = tr_ref[level, c ^ flip, i ^ flip].astype(F32)
            turned = roll64(piece)
            turned = jnp.where(lanes_low(piece.shape), -turned, turned)
            block = jnp.concatenate([piece, turned], axis=0).astype(BF16)
            w_ref[slot, i * 128 : (i + 1) * 128, c * 128 : (c + 1) * 128] = block
            across = roll64(jnp.concatenate([piece, turned], axis=0)).astype(BF16)
            w_ref[slot, i * 128 : (i + 1) * 128, 256 + c * 128 : 256 + (c + 1) * 128] = across


def split_factors(read16, fa_ref, fb_ref, first, rows):
    def body(step, carry):
        for part in range(SPLIT):
            at = pl.multiple_of(step * (16 * SPLIT) + part * 16, 16)
            fac = read16(at).astype(F32)
            turned = roll64(fac)
            low = lanes_low(fac.shape)
            fa_ref[pl.ds(first + at, 16), :] = jnp.where(low, fac, turned)
            fb_ref[pl.ds(first + at, 16), :] = jnp.where(low, -turned, fac)
        return carry

    lax.fori_loop(0, rows // (16 * SPLIT), body, 0)


def scaled(value, other, fa_ref, fb_ref, row):
    fa = fa_ref[pl.ds(row, 1), :]
    fb = fb_ref[pl.ds(row, 1), :]
    return (value * fa + other * fb).astype(BF16)


def gather16(rows_ref, index_ref, first):
    iota = lax.broadcasted_iota(jnp.int32, (8, 128), 0)
    halves = []
    for half in range(2):
        acc = None
        for i in range(8):
            at = index_ref[first + half * 8 + i]
            row = jnp.broadcast_to(rows_ref[pl.ds(at, 1), :], (8, 128))
            acc = row if acc is None else jnp.where(iota == i, row, acc)
        halves.append(acc)
    return jnp.concatenate(halves, axis=0).astype(BF16)


def pair_of(k, bit):
    low = k & (lax.shift_left(1, bit) - 1)
    first = lax.shift_left(lax.shift_right_logical(k, bit), bit + 1) | low
    return first, first + lax.shift_left(1, bit)


def source_kernel(
    dims, order_ref, bits_ref, ch_hbm, si_hbm, fac_hbm, tr_hbm, out_ref,
    ch_ref, si_ref, fac_ref, tr_ref, sems, x32, coef, mid_ref, fa, fb, w_ref,
):
    n_hi, n_lo, share, blocks, rhs = dims
    quarter = rhs // 4
    points = blocks * LEAF
    part = points // 4
    copies = [
        pltpu.make_async_copy(ch_hbm.at[pl.ds(i * part, part)], ch_ref.at[pl.ds(i * part, part)], sems.at[i])
        for i in range(4)
    ]
    copies.append(pltpu.make_async_copy(fac_hbm, fac_ref, sems.at[4]))
    copies.append(pltpu.make_async_copy(tr_hbm.at[pl.ds(0, 2)], tr_ref, sems.at[5]))
    copies.append(pltpu.make_async_copy(si_hbm, si_ref, sems.at[6]))
    for copy in copies:
        copy.start()

    def widen(step, carry):
        rows = pl.ds(pl.multiple_of(step * 512, 512), 512)
        x32[rows, :] = ch_ref[rows, :].astype(F32)
        return carry

    for i in range(4):
        copies[i].wait()
        lax.fori_loop(i * (part // 512), (i + 1) * (part // 512), widen, 0)
    for copy in copies[4:]:
        copy.wait()
    build_weights(w_ref, 0, tr_ref, 0)
    build_weights(w_ref, 1, tr_ref, 1)
    split_factors(lambda at: fac_ref[pl.ds(at, 16), :], fa, fb, 0, blocks * 8)

    def leaf(step, carry):
        for part in range(LEAVES):
            b = step * LEAVES + part
            first = pl.multiple_of(b * LEAF, LEAF)
            rows = jnp.concatenate([gather16(x32, order_ref, first + g * 16) for g in range(LEAF // 16)], axis=0)
            product = lax.dot_general(
                rows, si_ref[pl.ds(first, LEAF), :], (((0,), (0,)), ((), ())), preferred_element_type=F32
            )
            lower = roll64(product[rhs:])
            lower = jnp.where(lanes_low(lower.shape), -lower, lower)
            coef[b] = (product[:rhs] + lower).astype(BF16)
        return carry

    lax.fori_loop(0, blocks // LEAVES, leaf, 0)

    st, lm, hh = log2(share), log2(n_lo // 4), log2(n_hi // 2)

    def store_first(n, value):
        mid_ref[n] = value

    def store_second(n, value):
        t = n & (share - 1)
        core = (n >> st) & 1
        lmid = (n >> (st + 1)) & (n_lo // 4 - 1)
        z1 = (n >> (st + 1 + lm)) & 1
        rest = (n >> (st + 2 + lm)) & (n_hi // 2 - 1)
        y = n >> (st + 2 + lm + hh)
        target = rest * n_lo + core * (n_lo // 2) + lmid * 2
        m = (y * 2 + z1) * share + t
        for r in range(4):
            d = target + (r // 2) * (n_hi // 2) * n_lo + r % 2
            out_ref[d * (4 * share) + m] = value[r * quarter : (r + 1) * quarter]

    def level(index, src, store):
        bit = bits_ref[index]

        def body(step, carry):
            ends = [pair_of(step * SPAIRS + p, bit) for p in range(SPAIRS)]
            lhs = jnp.concatenate([jnp.concatenate([src[a], src[b]], axis=1) for a, b in ends], axis=0)
            res = jnp.dot(lhs, w_ref[index], preferred_element_type=F32)
            for p in range(SPAIRS):
                for c in range(2):
                    n = ends[p][c]
                    value = res[p * rhs : (p + 1) * rhs, c * 128 : (c + 1) * 128]
                    other = res[p * rhs : (p + 1) * rhs, 256 + c * 128 : 256 + (c + 1) * 128]
                    store(n, scaled(value, other, fa, fb, n * 8 + index))
            return carry

        lax.fori_loop(0, blocks // 2 // SPAIRS, body, 0)

    level(0, coef, store_first)
    level(1, mid_ref, store_second)


def spare_bit(bits_ref, dims):
    n_hi, n_lo, share, blocks, rhs = dims
    inner = log2(share) + log2(n_lo) - 1
    outer = log2(share) + log2(n_lo) + log2(n_hi) - 1
    free = [bit for bit in range(outer) if bit != inner][:3]
    spare = jnp.int32(free[2])
    for bit in (free[1], free[0]):
        taken = (bits_ref[2] == bit) | (bits_ref[3] == bit)
        spare = jnp.where(taken, spare, bit)
    return spare, inner, outer


def with_bit(i, bit, value):
    low = i & (lax.shift_left(1, bit) - 1)
    return lax.shift_left(lax.shift_right_logical(i, bit), bit + 1) | low | (value << bit)


def middle_kernel(dims, half, me_ref, bits_ref, g_ref, f0, f1, f2, f3, tr_ref, o0, o1, o2, o3, x, x2, fa, fb, w_ref):
    n_hi, n_lo, share, blocks, rhs = dims
    quarter = rhs // 4
    st = log2(share)
    y, core = me_ref[0], me_ref[1]
    spare, inner, outer = spare_bit(bits_ref, dims)
    count = blocks // 2
    for index in range(4):
        build_weights(w_ref, index, tr_ref, index + 2)
    build_weights(w_ref, 4, tr_ref, 6, core)
    build_weights(w_ref, 5, tr_ref, 7, y)
    low = lanes_low((8, 128))
    for j, f_ref in enumerate((f0, f1, f2, f3)):

        def split(step, carry, j=j, f_ref=f_ref):
            for part in range(32):
                i = step * 32 + part
                fac = f_ref[with_bit(i, spare, half)].astype(F32)
                turned = roll64(fac)
                rows = pl.ds(pl.multiple_of((j * count + i) * 8, 8), 8)
                fa[rows, :] = jnp.where(low, fac, turned)
                fb[rows, :] = jnp.where(low, -turned, fac)
            return carry

        lax.fori_loop(0, count // 32, split, 0)

    def read_arrived(j, i):
        n = with_bit(i, spare, half)
        first = (((j >> 1) ^ y) * 2 + ((j & 1) ^ core)) * share
        return g_ref[(n >> st) * (4 * share) + first + (n & (share - 1))]

    def held(x):
        def read(j, i):
            return x[j * count + i]

        return read

    def finish(res, p, c, row):
        value = res[p * quarter : (p + 1) * quarter, c * 128 : (c + 1) * 128]
        other = res[p * quarter : (p + 1) * quarter, 256 + c * 128 : 256 + (c + 1) * 128]
        return scaled(value, other, fa, fb, row)

    def level(index, bit, read, x):
        packed = bit - (bit > spare).astype(jnp.int32)
        ends = [pair_of(k, packed) for k in range(count // 2)]
        for j in range(4):
            lhs = jnp.concatenate([jnp.concatenate([read(j, a), read(j, b)], axis=1) for a, b in ends], axis=0)
            res = jnp.dot(lhs, w_ref[index - 2], preferred_element_type=F32)
            for p in range(count // 2):
                for c in range(2):
                    n = j * count + ends[p][c]
                    x[n] = finish(res, p, c, n * 8 + index)

    level(2, inner, read_arrived, x)
    level(3, outer, held(x), x2)
    level(4, bits_ref[2], held(x2), x)
    level(5, bits_ref[3], held(x), x2)

    def across(index, x, pairs, outs):
        for (a, b), (out_a, out_b) in zip(pairs, outs):
            lhs = jnp.concatenate(
                [x[pl.ds(j * count, count)].reshape(count * quarter, 128) for j in (a, b)], axis=1
            )
            res = jnp.dot(lhs, w_ref[index - 2], preferred_element_type=F32)
            for p in range(count):
                for c, (j, out) in enumerate(((a, out_a), (b, out_b))):
                    out[p] = finish(res, p, c, (j * count + p) * 8 + index)

    rest = [x.at[pl.ds(j * count, count)] for j in range(4)]
    across(6, x2, ((0, 1), (2, 3)), ((rest[0], rest[1]), (rest[2], rest[3])))
    across(7, x, ((0, 2), (1, 3)), ((o0, o2), (o1, o3)))


def receiver_values(dims, half, me_ref, bits_ref, ri_ref, pieces, stack, store):
    n_hi, n_lo, share, blocks, rhs = dims
    quarter = rhs // 4
    y, z1 = me_ref[0], me_ref[2]
    spare, _, _ = spare_bit(bits_ref, dims)

    def values(step, carry):
        for part in range(STACKS):
            i = step * STACKS + part
            for j, p_ref in enumerate(pieces):
                group = ((j >> 1) ^ y) * 2 + ((j & 1) ^ z1)
                at = pl.multiple_of(group * quarter, quarter)
                piece = p_ref[i].astype(F32)
                upper = jnp.where(lanes_low(piece.shape), piece, -piece)
                stack[part, pl.ds(at, quarter), :] = upper.astype(BF16)
                stack[part, pl.ds(at + rhs, quarter), :] = roll64(piece).astype(BF16)
            rows = pl.ds(pl.multiple_of(with_bit(i, spare, half) * LEAF, LEAF), LEAF)
            result = lax.dot_general(
                ri_ref[rows, :], stack[part], (((1,), (1,)), ((), ())), preferred_element_type=F32
            )
            store(i, rows, result)
        return carry

    lax.fori_loop(0, blocks // 2 // STACKS, values, 0)


def first_receivers(dims, me_ref, bits_ref, ri_ref, p0, p1, p2, p3, out_ref, stack):
    def store(i, rows, result):
        out_ref[pl.ds(pl.multiple_of(i * LEAF, LEAF), LEAF), :] = result.astype(BF16)

    receiver_values(dims, 0, me_ref, bits_ref, ri_ref, (p0, p1, p2, p3), stack, store)


def last_receivers(dims, me_ref, bits_ref, slot_ref, ri_ref, p0, p1, p2, p3, done_ref, out_ref, t32, stack):
    blocks = dims[3]
    points = blocks * LEAF

    spare, _, _ = spare_bit(bits_ref, dims)

    def store(i, rows, result):
        t32[rows, :] = result

    def widen(step, carry):
        for part in range(STACKS):
            i = step * STACKS + part
            held = done_ref[pl.ds(pl.multiple_of(i * LEAF, LEAF), LEAF), :]
            t32[pl.ds(pl.multiple_of(with_bit(i, spare, 0) * LEAF, LEAF), LEAF), :] = held.astype(F32)
        return carry

    lax.fori_loop(0, blocks // 2 // STACKS, widen, 0)
    receiver_values(dims, 1, me_ref, bits_ref, ri_ref, (p0, p1, p2, p3), stack, store)

    def pick(step, carry):
        for g in range(4):
            first = pl.multiple_of(step * 64 + g * 16, 16)
            out_ref[pl.ds(first, 16), :] = gather16(t32, slot_ref, first)
        return carry

    lax.fori_loop(0, points // 64, pick, 0)


def on_vmem():
    return pl.BlockSpec(memory_space=pltpu.VMEM)


def on_any():
    return pl.BlockSpec(memory_space=pl.ANY)


def on_smem():
    return pl.BlockSpec(memory_space=pltpu.SMEM)


def params(mebibytes):
    return pltpu.CompilerParams(vmem_limit_bytes=mebibytes * 2**20)


def per_device(
    n_hi, n_lo, charges, source_order, source_interp, factors, transfers, level_bits, receiver_interp, receiver_slot
):
    points, twice_rhs = charges.shape
    rhs = twice_rhs // 2
    blocks = points // LEAF
    devices = n_hi * n_lo
    share = blocks // devices
    quarter = rhs // 4
    dims = (n_hi, n_lo, share, blocks, rhs)
    half_hi, half_lo = n_hi // 2 * n_lo, n_lo // 2
    hi, lo = lax.axis_index("hi"), lax.axis_index("lo")
    me = jnp.stack([hi >> (log2(n_hi) - 1), lo & 1, lo >> (log2(n_lo) - 1), hi, lo]).astype(jnp.int32)

    def swapped(device, j):
        flipped = device ^ (half_hi if j >> 1 else 0)
        core, top = flipped & 1, (flipped // half_lo) & 1
        base = flipped - core - top * half_lo
        return base + (core ^ (j & 1)) * half_lo + top

    spread = factors.reshape(n_hi, 2, n_lo // 4, 2, share, 8, 128).transpose(0, 3, 2, 1, 4, 5, 6)
    spread = lax.all_to_all(spread.reshape(blocks, 8, 128), AXES, split_axis=0, concat_axis=0, tiled=True)
    facs = [spread]
    for j in range(1, 4):
        mask = (half_hi if j >> 1 else 0) ^ (j & 1)
        facs.append(lax.ppermute(spread, AXES, [(s, s ^ mask) for s in range(devices)]))

    sent = pl.pallas_call(
        functools.partial(source_kernel, dims),
        out_shape=jax.ShapeDtypeStruct((devices * 4 * share, quarter, 128), BF16),
        in_specs=[on_smem(), on_smem()] + [on_any()] * 4,
        out_specs=on_vmem(),
        scratch_shapes=[
            pltpu.VMEM((points, 128), BF16),
            pltpu.VMEM((points, 128), BF16),
            pltpu.VMEM((blocks * 8, 128), BF16),
            pltpu.VMEM((2,) + transfers.shape[1:], BF16),
            pltpu.SemaphoreType.DMA((7,)),
            pltpu.VMEM((points, 128), F32),
            pltpu.VMEM((blocks, rhs, 128), BF16),
            pltpu.VMEM((blocks, rhs, 128), BF16),
            pltpu.VMEM((blocks * 8, 128), F32),
            pltpu.VMEM((blocks * 8, 128), F32),
            pltpu.VMEM((2, 256, 512), BF16),
        ],
        compiler_params=params(60),
        name="source_side",
    )(source_order, level_bits, charges, source_interp, factors.reshape(blocks * 8, 128), transfers)

    arrived = lax.all_to_all(sent, AXES, split_axis=0, concat_axis=0, tiled=True)

    piece = jax.ShapeDtypeStruct((blocks // 2, quarter, 128), BF16)
    homes = []
    for half in range(2):
        pieces = pl.pallas_call(
            functools.partial(middle_kernel, dims, half),
            out_shape=[piece] * 4,
            in_specs=[on_smem(), on_smem()] + [on_vmem()] * 6,
            out_specs=[on_vmem()] * 4,
            scratch_shapes=[
                pltpu.VMEM((2 * blocks, quarter, 128), BF16),
                pltpu.VMEM((2 * blocks, quarter, 128), BF16),
                pltpu.VMEM((2 * blocks * 8, 128), F32),
                pltpu.VMEM((2 * blocks * 8, 128), F32),
                pltpu.VMEM((6, 256, 512), BF16),
            ],
            compiler_params=params(16),
            name="middle_levels",
        )(me, level_bits, arrived, *facs, transfers)
        homes.append(
            [lax.ppermute(pieces[j], AXES, [(s, swapped(s, j)) for s in range(devices)]) for j in range(4)]
        )

    done = pl.pallas_call(
        functools.partial(first_receivers, dims),
        out_shape=jax.ShapeDtypeStruct((points // 2, twice_rhs), BF16),
        in_specs=[on_smem(), on_smem()] + [on_vmem()] * 5,
        out_specs=on_vmem(),
        scratch_shapes=[pltpu.VMEM((STACKS, 2 * rhs, 128), BF16)],
        compiler_params=params(16),
        name="first_receivers",
    )(me, level_bits, receiver_interp, *homes[0])
    return pl.pallas_call(
        functools.partial(last_receivers, dims),
        out_shape=jax.ShapeDtypeStruct((points, twice_rhs), BF16),
        in_specs=[on_smem(), on_smem(), on_smem()] + [on_vmem()] * 6,
        out_specs=on_vmem(),
        scratch_shapes=[pltpu.VMEM((points, 128), F32), pltpu.VMEM((STACKS, 2 * rhs, 128), BF16)],
        compiler_params=params(20),
        name="last_receivers",
    )(me, level_bits, receiver_slot, receiver_interp, *homes[1], done)


def solution(mesh):
    body = functools.partial(per_device, mesh.shape["hi"], mesh.shape["lo"])
    return jax.shard_map(
        body,
        mesh=mesh,
        in_specs=(
            P(AXES, None),
            P(AXES),
            P(AXES, None),
            P(AXES, None, None),
            P(),
            P(),
            P(AXES, None),
            P(AXES),
        ),
        out_specs=P(AXES, None),
        check_vma=False,
    )
```

```python
import functools

import jax
import jax.numpy as jnp
from jax import lax
from jax.experimental import pallas as pl
from jax.experimental.pallas import tpu as pltpu
from jax.sharding import PartitionSpec as P

LEAF = 64
AXES = ("hi", "lo")
SPLIT = 16
STACKS = 16
QUARTERS = ((0,), (1, 2), (3,))
LEAVES = 32
SPAIRS = 32
F32 = jnp.float32
BF16 = jnp.bfloat16


def log2(value):
    return value.bit_length() - 1


def lanes_low(shape):
    return lax.broadcasted_iota(jnp.int32, shape, len(shape) - 1) < 64


def roll64(value):
    return pltpu.roll(value, 64, 1)


def build_weights(w_ref, slot, tr_ref, level, flip=0):
    for i in range(2):
        for c in range(2):
            piece = tr_ref[level, c ^ flip, i ^ flip].astype(F32)
            turned = roll64(piece)
            turned = jnp.where(lanes_low(piece.shape), -turned, turned)
            block = jnp.concatenate([piece, turned], axis=0).astype(BF16)
            w_ref[slot, i * 128 : (i + 1) * 128, c * 128 : (c + 1) * 128] = block
            across = roll64(jnp.concatenate([piece, turned], axis=0)).astype(BF16)
            w_ref[slot, i * 128 : (i + 1) * 128, 256 + c * 128 : 256 + (c + 1) * 128] = across


def split_factors(read16, fa_ref, fb_ref, first, rows):
    def body(step, carry):
        for part in range(SPLIT):
            at = pl.multiple_of(step * (16 * SPLIT) + part * 16, 16)
            fac = read16(at).astype(F32)
            turned = roll64(fac)
            low = lanes_low(fac.shape)
            fa_ref[pl.ds(first + at, 16), :] = jnp.where(low, fac, turned)
            fb_ref[pl.ds(first + at, 16), :] = jnp.where(low, -turned, fac)
        return carry

    lax.fori_loop(0, rows // (16 * SPLIT), body, 0)


def scaled(value, other, fa_ref, fb_ref, row):
    fa = fa_ref[pl.ds(row, 1), :]
    fb = fb_ref[pl.ds(row, 1), :]
    return (value * fa + other * fb).astype(BF16)


def gather16(rows_ref, index_ref, first):
    iota = lax.broadcasted_iota(jnp.int32, (8, 128), 0)
    halves = []
    for half in range(2):
        acc = None
        for i in range(8):
            at = index_ref[first + half * 8 + i]
            row = jnp.broadcast_to(rows_ref[pl.ds(at, 1), :], (8, 128))
            acc = row if acc is None else jnp.where(iota == i, row, acc)
        halves.append(acc)
    return jnp.concatenate(halves, axis=0).astype(BF16)


def pair_of(k, bit):
    low = k & (lax.shift_left(1, bit) - 1)
    first = lax.shift_left(lax.shift_right_logical(k, bit), bit + 1) | low
    return first, first + lax.shift_left(1, bit)


def source_kernel(
    dims, order_ref, bits_ref, ch_hbm, si_hbm, fac_hbm, tr_hbm, out_ref,
    ch_ref, si_ref, fac_ref, tr_ref, sems, x32, mid_ref, fa, fb, w_ref,
):
    n_hi, n_lo, share, blocks, rhs = dims
    quarter = rhs // 4
    points = blocks * LEAF
    part = points // 4
    copies = [
        pltpu.make_async_copy(ch_hbm.at[pl.ds(i * part, part)], ch_ref.at[pl.ds(i * part, part)], sems.at[i])
        for i in range(4)
    ]
    copies.append(pltpu.make_async_copy(fac_hbm, fac_ref, sems.at[4]))
    copies.append(pltpu.make_async_copy(tr_hbm.at[pl.ds(0, 2)], tr_ref, sems.at[5]))
    copies.append(pltpu.make_async_copy(si_hbm, si_ref, sems.at[6]))
    for copy in copies[4:6] + copies[:4] + copies[6:]:
        copy.start()
    copies[5].wait()
    build_weights(w_ref, 0, tr_ref, 0)
    build_weights(w_ref, 1, tr_ref, 1)
    copies[4].wait()
    split_factors(lambda at: fac_ref[pl.ds(at, 16), :], fa, fb, 0, blocks * 8)

    def widen(step, carry):
        rows = pl.ds(pl.multiple_of(step * 512, 512), 512)
        x32[rows, :] = ch_ref[rows, :].astype(F32)
        return carry

    for i in range(4):
        copies[i].wait()
        lax.fori_loop(i * (part // 512), (i + 1) * (part // 512), widen, 0)
    copies[6].wait()

    def leaf(b):
        first = pl.multiple_of(b * LEAF, LEAF)
        rows = jnp.concatenate([gather16(x32, order_ref, first + g * 16) for g in range(LEAF // 16)], axis=0)
        product = lax.dot_general(
            rows, si_ref[pl.ds(first, LEAF), :], (((0,), (0,)), ((), ())), preferred_element_type=F32
        )
        lower = roll64(product[rhs:])
        lower = jnp.where(lanes_low(lower.shape), -lower, lower)
        return (product[:rhs] + lower).astype(BF16)

    def level(index, pairs, read, store):
        bit = bits_ref[index]

        def body(step, carry):
            ends = [pair_of(step * pairs + p, bit) for p in range(pairs)]
            lhs = jnp.concatenate([jnp.concatenate([read(a), read(b)], axis=1) for a, b in ends], axis=0)
            res = jnp.dot(lhs, w_ref[index], preferred_element_type=F32)
            for p in range(pairs):
                for c in range(2):
                    n = ends[p][c]
                    value = res[p * rhs : (p + 1) * rhs, c * 128 : (c + 1) * 128]
                    other = res[p * rhs : (p + 1) * rhs, 256 + c * 128 : 256 + (c + 1) * 128]
                    store(n, scaled(value, other, fa, fb, n * 8 + index))
            return carry

        lax.fori_loop(0, blocks // 2 // pairs, body, 0)

    st, lm, hh = log2(share), log2(n_lo // 4), log2(n_hi // 2)

    def store_first(n, value):
        mid_ref[n] = value

    def store_second(n, value):
        t = n & (share - 1)
        core = (n >> st) & 1
        lmid = (n >> (st + 1)) & (n_lo // 4 - 1)
        z1 = (n >> (st + 1 + lm)) & 1
        rest = (n >> (st + 2 + lm)) & (n_hi // 2 - 1)
        y = n >> (st + 2 + lm + hh)
        target = rest * n_lo + core * (n_lo // 2) + lmid * 2
        m = (y * 2 + z1) * share + t
        for r in range(4):
            d = target + (r // 2) * (n_hi // 2) * n_lo + r % 2
            out_ref[d * (4 * share) + m] = value[r * quarter : (r + 1) * quarter]

    level(0, LEAVES // 2, leaf, store_first)
    level(1, SPAIRS, lambda n: mid_ref[n], store_second)


def spare_bits(bits_ref, dims):
    n_hi, n_lo, share, blocks, rhs = dims
    inner = log2(share) + log2(n_lo) - 1
    outer = log2(share) + log2(n_lo) + log2(n_hi) - 1
    free = [bit for bit in range(outer) if bit != inner]

    def first_free(after):
        found = jnp.int32(free[-1])
        for bit in reversed(free[:-1]):
            usable = (bits_ref[2] != bit) & (bits_ref[3] != bit) & (bit > after)
            found = jnp.where(usable, bit, found)
        return found

    first = first_free(-1)
    return (first, first_free(first)), inner, outer


def with_bit(i, bit, value):
    low = i & (lax.shift_left(1, bit) - 1)
    return lax.shift_left(lax.shift_right_logical(i, bit), bit + 1) | low | (value << bit)


def in_quarter(i, spare, quarter):
    return with_bit(with_bit(i, spare[0], quarter & 1), spare[1], quarter >> 1)


def inverse_kernel(dims, slot_ref, after_ref, inverse_ref):
    def invert(step, carry):
        for part in range(32):
            at = step * 32 + part
            inverse_ref[slot_ref[at]] = at
        return carry

    lax.fori_loop(0, dims[3] * LEAF // 32, invert, 0)


def middle_kernel(
    dims, quarters, me_ref, bits_ref, g_ref, f0, f1, f2, f3, tr_ref, o0, o1, o2, o3, x, x2, fa, fb, w_ref
):
    n_hi, n_lo, share, blocks, rhs = dims
    rows = rhs // 4
    st = log2(share)
    y, core = me_ref[0], me_ref[1]
    spare, inner, outer = spare_bits(bits_ref, dims)
    count = blocks // 4
    low = lanes_low((8, 128))
    for index in range(4):
        build_weights(w_ref, index, tr_ref, index + 2)
    build_weights(w_ref, 4, tr_ref, 6, core)
    build_weights(w_ref, 5, tr_ref, 7, y)

    def finish(res, p, c, row):
        value = res[p * rows : (p + 1) * rows, c * 128 : (c + 1) * 128]
        other = res[p * rows : (p + 1) * rows, 256 + c * 128 : 256 + (c + 1) * 128]
        return scaled(value, other, fa, fb, row)

    def held(x):
        def read(j, i):
            return x[j * count + i]

        return read

    def level(index, bit, read, x):
        packed = bit - (bit > spare[0]).astype(jnp.int32) - (bit > spare[1]).astype(jnp.int32)
        ends = [pair_of(k, packed) for k in range(count // 2)]
        for j in range(4):
            lhs = jnp.concatenate([jnp.concatenate([read(j, a), read(j, b)], axis=1) for a, b in ends], axis=0)
            res = jnp.dot(lhs, w_ref[index - 2], preferred_element_type=F32)
            for p in range(count // 2):
                for c in range(2):
                    n = j * count + ends[p][c]
                    x[n] = finish(res, p, c, n * 8 + index)

    def across(index, x, pairs, outs):
        for (a, b), (out_a, out_b) in zip(pairs, outs):
            lhs = jnp.concatenate([x[pl.ds(j * count, count)].reshape(count * rows, 128) for j in (a, b)], axis=1)
            res = jnp.dot(lhs, w_ref[index - 2], preferred_element_type=F32)
            for p in range(count):
                for c, (j, out) in enumerate(((a, out_a), (b, out_b))):
                    out[p] = finish(res, p, c, (j * count + p) * 8 + index)

    for place, quarter in enumerate(quarters):
        for j, f_ref in enumerate((f0, f1, f2, f3)):
            for i in range(count):
                fac = f_ref[in_quarter(i, spare, quarter)].astype(F32)
                turned = roll64(fac)
                at = pl.ds((j * count + i) * 8, 8)
                fa[at, :] = jnp.where(low, fac, turned)
                fb[at, :] = jnp.where(low, -turned, fac)

        def read_arrived(j, i):
            n = in_quarter(i, spare, quarter)
            first = (((j >> 1) ^ y) * 2 + ((j & 1) ^ core)) * share
            return g_ref[(n >> st) * (4 * share) + first + (n & (share - 1))]

        level(2, inner, read_arrived, x)
        level(3, outer, held(x), x2)
        level(4, bits_ref[2], held(x2), x)
        level(5, bits_ref[3], held(x), x2)
        rest = [x.at[pl.ds(j * count, count)] for j in range(4)]
        done = [o.at[pl.ds(place * count, count)] for o in (o0, o1, o2, o3)]
        across(6, x2, ((0, 1), (2, 3)), ((rest[0], rest[1]), (rest[2], rest[3])))
        across(7, x, ((0, 2), (1, 3)), ((done[0], done[2]), (done[1], done[3])))


def receive(dims, quarters, me_ref, bits_ref, inverse_ref, ri_ref, pieces, out32, stack, t32):
    n_hi, n_lo, share, blocks, rhs = dims
    part_rows = rhs // 4
    y, z1 = me_ref[0], me_ref[2]
    spare, _, _ = spare_bits(bits_ref, dims)
    count = blocks // 4
    lows = lanes_low((part_rows, 128))

    for place, quarter in enumerate(quarters):

        def body(step, carry):
            for part in range(STACKS):
                i = step * STACKS + part
                n = in_quarter(i, spare, quarter)
                for j, p_ref in enumerate(pieces):
                    group = ((j >> 1) ^ y) * 2 + ((j & 1) ^ z1)
                    at = pl.multiple_of(group * part_rows, part_rows)
                    piece = p_ref[place * count + i].astype(F32)
                    stack[part, pl.ds(at, part_rows), :] = jnp.where(lows, piece, -piece).astype(BF16)
                    stack[part, pl.ds(at + rhs, part_rows), :] = roll64(piece).astype(BF16)
                first = pl.multiple_of(n * LEAF, LEAF)
                t32[part * LEAF : (part + 1) * LEAF, :] = lax.dot_general(
                    ri_ref[pl.ds(first, LEAF), :],
                    stack[part],
                    (((1,), (1,)), ((), ())),
                    preferred_element_type=F32,
                )
                for r in range(LEAF):
                    out32[pl.ds(inverse_ref[first + r], 1), :] = t32[part * LEAF + r : part * LEAF + r + 1, :]
            return carry

        lax.fori_loop(0, count // STACKS, body, 0)


def first_receivers(dims, me_ref, bits_ref, inverse_ref, ri_ref, *refs):
    pieces, (out_ref, stack, t32) = refs[:-3], refs[-3:]
    for at, quarters in enumerate(QUARTERS[:-1]):
        receive(
            dims, quarters, me_ref, bits_ref, inverse_ref, ri_ref, pieces[4 * at : 4 * at + 4], out_ref, stack, t32
        )


def last_receivers(dims, me_ref, bits_ref, inverse_ref, ri_ref, p0, p1, p2, p3, done_ref, out_hbm, whole, narrow, sems, stack, t32):
    points = dims[3] * LEAF
    part = points // 4

    def take(step, carry):
        rows = pl.ds(pl.multiple_of(step * 512, 512), 512)
        whole[rows, :] = done_ref[rows, :]
        return carry

    lax.fori_loop(0, points // 512, take, 0)
    receive(dims, QUARTERS[-1], me_ref, bits_ref, inverse_ref, ri_ref, (p0, p1, p2, p3), whole, stack, t32)
    copies = []
    for i in range(4):

        def round_off(step, carry):
            rows = pl.ds(pl.multiple_of(step * 512, 512), 512)
            narrow[rows, :] = whole[rows, :].astype(BF16)
            return carry

        lax.fori_loop(i * (part // 512), (i + 1) * (part // 512), round_off, 0)
        rows = pl.ds(i * part, part)
        copies.append(pltpu.make_async_copy(narrow.at[rows], out_hbm.at[rows], sems.at[i]))
        copies[-1].start()
    for copy in copies:
        copy.wait()


def on_vmem():
    return pl.BlockSpec(memory_space=pltpu.VMEM)


def on_any():
    return pl.BlockSpec(memory_space=pl.ANY)


def on_smem():
    return pl.BlockSpec(memory_space=pltpu.SMEM)


def params(mebibytes):
    return pltpu.CompilerParams(vmem_limit_bytes=mebibytes * 2**20)


def per_device(
    n_hi, n_lo, charges, source_order, source_interp, factors, transfers, level_bits, receiver_interp, receiver_slot
):
    points, twice_rhs = charges.shape
    rhs = twice_rhs // 2
    blocks = points // LEAF
    devices = n_hi * n_lo
    share = blocks // devices
    quarter = rhs // 4
    dims = (n_hi, n_lo, share, blocks, rhs)
    half_hi, half_lo = n_hi // 2 * n_lo, n_lo // 2
    hi, lo = lax.axis_index("hi"), lax.axis_index("lo")
    me = jnp.stack([hi >> (log2(n_hi) - 1), lo & 1, lo >> (log2(n_lo) - 1), hi, lo]).astype(jnp.int32)

    def swapped(device, j):
        flipped = device ^ (half_hi if j >> 1 else 0)
        core, top = flipped & 1, (flipped // half_lo) & 1
        base = flipped - core - top * half_lo
        return base + (core ^ (j & 1)) * half_lo + top

    spread = factors.reshape(n_hi, 2, n_lo // 4, 2, share, 8, 128).transpose(0, 3, 2, 1, 4, 5, 6)
    spread = lax.all_to_all(spread.reshape(blocks, 8, 128), AXES, split_axis=0, concat_axis=0, tiled=True)
    facs = [spread]
    for j in range(1, 4):
        mask = (half_hi if j >> 1 else 0) ^ (j & 1)
        facs.append(lax.ppermute(spread, AXES, [(s, s ^ mask) for s in range(devices)]))

    sent = pl.pallas_call(
        functools.partial(source_kernel, dims),
        out_shape=jax.ShapeDtypeStruct((devices * 4 * share, quarter, 128), BF16),
        in_specs=[on_smem(), on_smem()] + [on_any()] * 4,
        out_specs=on_vmem(),
        scratch_shapes=[
            pltpu.VMEM((points, 128), BF16),
            pltpu.VMEM((points, 128), BF16),
            pltpu.VMEM((blocks * 8, 128), BF16),
            pltpu.VMEM((2,) + transfers.shape[1:], BF16),
            pltpu.SemaphoreType.DMA((7,)),
            pltpu.VMEM((points, 128), F32),
            pltpu.VMEM((blocks, rhs, 128), BF16),
            pltpu.VMEM((blocks * 8, 128), F32),
            pltpu.VMEM((blocks * 8, 128), F32),
            pltpu.VMEM((2, 256, 512), BF16),
        ],
        compiler_params=params(60),
        name="source_side",
    )(source_order, level_bits, charges, source_interp, factors.reshape(blocks * 8, 128), transfers)

    arrived = lax.all_to_all(sent, AXES, split_axis=0, concat_axis=0, tiled=True)

    inverse = pl.pallas_call(
        functools.partial(inverse_kernel, dims),
        out_shape=jax.ShapeDtypeStruct((points,), jnp.int32),
        in_specs=[on_smem(), on_any()],
        out_specs=on_smem(),
        compiler_params=params(12),
        cost_estimate=pl.CostEstimate(flops=10**10, bytes_accessed=2**25, transcendentals=0),
        name="inverse_slots",
    )(receiver_slot, facs[3])
    facs[1], inverse = lax.optimization_barrier((facs[1], inverse))

    homes = []
    for quarters in QUARTERS:
        count = len(quarters) * blocks // 4
        pieces = pl.pallas_call(
            functools.partial(middle_kernel, dims, quarters),
            out_shape=[jax.ShapeDtypeStruct((count, quarter, 128), BF16)] * 4,
            in_specs=[on_smem(), on_smem()] + [on_vmem()] * 6,
            out_specs=[on_vmem()] * 4,
            scratch_shapes=[
                pltpu.VMEM((blocks, quarter, 128), BF16),
                pltpu.VMEM((blocks, quarter, 128), BF16),
                pltpu.VMEM((blocks * 8, 128), F32),
                pltpu.VMEM((blocks * 8, 128), F32),
                pltpu.VMEM((6, 256, 512), BF16),
            ],
            compiler_params=params(16),
            name="middle_levels",
        )(me, level_bits, arrived, *facs, transfers)
        homes.append(
            [lax.ppermute(pieces[j], AXES, [(s, swapped(s, j)) for s in range(devices)]) for j in range(4)]
        )

    work = [pltpu.VMEM((STACKS, 2 * rhs, 128), BF16), pltpu.VMEM((STACKS * LEAF, 128), F32)]
    done = pl.pallas_call(
        functools.partial(first_receivers, dims),
        out_shape=jax.ShapeDtypeStruct((points, twice_rhs), F32),
        in_specs=[on_smem(), on_smem(), on_smem()] + [on_vmem()] * (4 * len(QUARTERS) - 3),
        out_specs=on_vmem(),
        scratch_shapes=work,
        compiler_params=params(16),
        name="first_receivers",
    )(me, level_bits, inverse, receiver_interp, *[piece for home in homes[:-1] for piece in home])
    return pl.pallas_call(
        functools.partial(last_receivers, dims),
        out_shape=jax.ShapeDtypeStruct((points, twice_rhs), BF16),
        in_specs=[on_smem(), on_smem(), on_smem()] + [on_vmem()] * 6,
        out_specs=on_any(),
        scratch_shapes=[
            pltpu.VMEM((points, 128), F32),
            pltpu.VMEM((points, 128), BF16),
            pltpu.SemaphoreType.DMA((4,)),
        ]
        + work,
        compiler_params=params(24),
        name="last_receivers",
    )(me, level_bits, inverse, receiver_interp, *homes[-1], done)


def solution(mesh):
    body = functools.partial(per_device, mesh.shape["hi"], mesh.shape["lo"])
    return jax.shard_map(
        body,
        mesh=mesh,
        in_specs=(
            P(AXES, None),
            P(AXES),
            P(AXES, None),
            P(AXES, None, None),
            P(),
            P(),
            P(AXES, None),
            P(AXES),
        ),
        out_specs=P(AXES, None),
        check_vma=False,
    )
```

```python
import functools

import jax
import jax.numpy as jnp
from jax import lax
from jax.experimental import pallas as pl
from jax.experimental.pallas import tpu as pltpu
from jax.sharding import PartitionSpec as P

LEAF = 64
AXES = ("hi", "lo")
SPLIT = 16
STACKS = 16
QUARTERS = ((0,), (1,), (2,), (3,))
LEAVES = 32
SPAIRS = 32
F32 = jnp.float32
BF16 = jnp.bfloat16


def log2(value):
    return value.bit_length() - 1


def lanes_low(shape):
    return lax.broadcasted_iota(jnp.int32, shape, len(shape) - 1) < 64


def roll64(value):
    return pltpu.roll(value, 64, 1)


def build_weights(w_ref, slot, tr_ref, level, flip=0):
    for i in range(2):
        for c in range(2):
            piece = tr_ref[level, c ^ flip, i ^ flip].astype(F32)
            turned = roll64(piece)
            turned = jnp.where(lanes_low(piece.shape), -turned, turned)
            block = jnp.concatenate([piece, turned], axis=0).astype(BF16)
            w_ref[slot, i * 128 : (i + 1) * 128, c * 128 : (c + 1) * 128] = block
            across = roll64(jnp.concatenate([piece, turned], axis=0)).astype(BF16)
            w_ref[slot, i * 128 : (i + 1) * 128, 256 + c * 128 : 256 + (c + 1) * 128] = across


def split_factors(read16, fa_ref, fb_ref, first, rows):
    def body(step, carry):
        for part in range(SPLIT):
            at = pl.multiple_of(step * (16 * SPLIT) + part * 16, 16)
            fac = read16(at).astype(F32)
            turned = roll64(fac)
            low = lanes_low(fac.shape)
            fa_ref[pl.ds(first + at, 16), :] = jnp.where(low, fac, turned)
            fb_ref[pl.ds(first + at, 16), :] = jnp.where(low, -turned, fac)
        return carry

    lax.fori_loop(0, rows // (16 * SPLIT), body, 0)


def scaled(value, other, fa_ref, fb_ref, row):
    fa = fa_ref[pl.ds(row, 1), :]
    fb = fb_ref[pl.ds(row, 1), :]
    return (value * fa + other * fb).astype(BF16)


def gather16(rows_ref, index_ref, first):
    iota = lax.broadcasted_iota(jnp.int32, (8, 128), 0)
    halves = []
    for half in range(2):
        acc = None
        for i in range(8):
            at = index_ref[first + half * 8 + i]
            row = jnp.broadcast_to(rows_ref[pl.ds(at, 1), :], (8, 128))
            acc = row if acc is None else jnp.where(iota == i, row, acc)
        halves.append(acc)
    return jnp.concatenate(halves, axis=0).astype(BF16)


def pair_of(k, bit):
    low = k & (lax.shift_left(1, bit) - 1)
    first = lax.shift_left(lax.shift_right_logical(k, bit), bit + 1) | low
    return first, first + lax.shift_left(1, bit)


def source_kernel(
    dims, order_hbm, bits_ref, ch_hbm, si_hbm, fac_hbm, tr_hbm, out_ref,
    order_ref, ch_ref, si_ref, fac_ref, tr_ref, sems, x32, mid_ref, fa, fb, w_ref,
):
    n_hi, n_lo, share, blocks, rhs = dims
    quarter = rhs // 4
    points = blocks * LEAF
    part = points // 4
    copies = [
        pltpu.make_async_copy(ch_hbm.at[pl.ds(i * part, part)], ch_ref.at[pl.ds(i * part, part)], sems.at[i])
        for i in range(4)
    ]
    copies.append(pltpu.make_async_copy(fac_hbm, fac_ref, sems.at[4]))
    copies.append(pltpu.make_async_copy(tr_hbm.at[pl.ds(0, 2)], tr_ref, sems.at[5]))
    copies.append(pltpu.make_async_copy(si_hbm, si_ref, sems.at[6]))
    copies.append(pltpu.make_async_copy(order_hbm, order_ref, sems.at[7]))
    for copy in copies[4:6] + copies[:4] + copies[6:]:
        copy.start()
    copies[5].wait()
    build_weights(w_ref, 0, tr_ref, 0)
    build_weights(w_ref, 1, tr_ref, 1)
    copies[4].wait()
    split_factors(lambda at: fac_ref[pl.ds(at, 16), :], fa, fb, 0, blocks * 8)

    def widen(step, carry):
        rows = pl.ds(pl.multiple_of(step * 512, 512), 512)
        x32[rows, :] = ch_ref[rows, :].astype(F32)
        return carry

    for i in range(4):
        copies[i].wait()
        lax.fori_loop(i * (part // 512), (i + 1) * (part // 512), widen, 0)
    copies[6].wait()
    copies[7].wait()

    def leaf(b):
        first = pl.multiple_of(b * LEAF, LEAF)
        rows = jnp.concatenate([gather16(x32, order_ref, first + g * 16) for g in range(LEAF // 16)], axis=0)
        product = lax.dot_general(
            rows, si_ref[pl.ds(first, LEAF), :], (((0,), (0,)), ((), ())), preferred_element_type=F32
        )
        lower = roll64(product[rhs:])
        lower = jnp.where(lanes_low(lower.shape), -lower, lower)
        return (product[:rhs] + lower).astype(BF16)

    def level(index, pairs, read, store):
        bit = bits_ref[index]

        def body(step, carry):
            ends = [pair_of(step * pairs + p, bit) for p in range(pairs)]
            lhs = jnp.concatenate([jnp.concatenate([read(a), read(b)], axis=1) for a, b in ends], axis=0)
            res = jnp.dot(lhs, w_ref[index], preferred_element_type=F32)
            for p in range(pairs):
                for c in range(2):
                    n = ends[p][c]
                    value = res[p * rhs : (p + 1) * rhs, c * 128 : (c + 1) * 128]
                    other = res[p * rhs : (p + 1) * rhs, 256 + c * 128 : 256 + (c + 1) * 128]
                    store(n, scaled(value, other, fa, fb, n * 8 + index))
            return carry

        lax.fori_loop(0, blocks // 2 // pairs, body, 0)

    st, lm, hh = log2(share), log2(n_lo // 4), log2(n_hi // 2)

    def store_first(n, value):
        mid_ref[n] = value

    def store_second(n, value):
        t = n & (share - 1)
        core = (n >> st) & 1
        lmid = (n >> (st + 1)) & (n_lo // 4 - 1)
        z1 = (n >> (st + 1 + lm)) & 1
        rest = (n >> (st + 2 + lm)) & (n_hi // 2 - 1)
        y = n >> (st + 2 + lm + hh)
        target = rest * n_lo + core * (n_lo // 2) + lmid * 2
        m = (y * 2 + z1) * share + t
        for r in range(4):
            d = target + (r // 2) * (n_hi // 2) * n_lo + r % 2
            out_ref[d * (4 * share) + m] = value[r * quarter : (r + 1) * quarter]

    level(0, LEAVES // 2, leaf, store_first)
    level(1, SPAIRS, lambda n: mid_ref[n], store_second)


def spare_bits(bits_ref, dims):
    n_hi, n_lo, share, blocks, rhs = dims
    inner = log2(share) + log2(n_lo) - 1
    outer = log2(share) + log2(n_lo) + log2(n_hi) - 1
    free = [bit for bit in range(outer) if bit != inner]

    def first_free(after):
        found = jnp.int32(free[-1])
        for bit in reversed(free[:-1]):
            usable = (bits_ref[2] != bit) & (bits_ref[3] != bit) & (bit > after)
            found = jnp.where(usable, bit, found)
        return found

    first = first_free(-1)
    return (first, first_free(first)), inner, outer


def with_bit(i, bit, value):
    low = i & (lax.shift_left(1, bit) - 1)
    return lax.shift_left(lax.shift_right_logical(i, bit), bit + 1) | low | (value << bit)


def in_quarter(i, spare, quarter):
    return with_bit(with_bit(i, spare[0], quarter & 1), spare[1], quarter >> 1)


def inverse_kernel(dims, slot_ref, after_ref, inverse_ref):
    def invert(step, carry):
        for part in range(32):
            at = step * 32 + part
            inverse_ref[slot_ref[at]] = at
        return carry

    lax.fori_loop(0, dims[3] * LEAF // 32, invert, 0)


def middle_kernel(
    dims, quarters, me_ref, bits_ref, g_ref, f0, f1, f2, f3, tr_ref, after_ref, o0, o1, o2, o3, x, x2, fa, fb, w_ref
):
    n_hi, n_lo, share, blocks, rhs = dims
    rows = rhs // 4
    st = log2(share)
    y, core = me_ref[0], me_ref[1]
    spare, inner, outer = spare_bits(bits_ref, dims)
    count = blocks // 4
    low = lanes_low((8, 128))
    for index in range(4):
        build_weights(w_ref, index, tr_ref, index + 2)
    build_weights(w_ref, 4, tr_ref, 6, core)
    build_weights(w_ref, 5, tr_ref, 7, y)

    def finish(res, p, c, row):
        value = res[p * rows : (p + 1) * rows, c * 128 : (c + 1) * 128]
        other = res[p * rows : (p + 1) * rows, 256 + c * 128 : 256 + (c + 1) * 128]
        return scaled(value, other, fa, fb, row)

    def held(x):
        def read(j, i):
            return x[j * count + i]

        return read

    def level(index, bit, read, x):
        packed = bit - (bit > spare[0]).astype(jnp.int32) - (bit > spare[1]).astype(jnp.int32)
        ends = [pair_of(k, packed) for k in range(count // 2)]
        for j in range(4):
            lhs = jnp.concatenate([jnp.concatenate([read(j, a), read(j, b)], axis=1) for a, b in ends], axis=0)
            res = jnp.dot(lhs, w_ref[index - 2], preferred_element_type=F32)
            for p in range(count // 2):
                for c in range(2):
                    n = j * count + ends[p][c]
                    x[n] = finish(res, p, c, n * 8 + index)

    def across(index, x, pairs, outs):
        for (a, b), (out_a, out_b) in zip(pairs, outs):
            lhs = jnp.concatenate([x[pl.ds(j * count, count)].reshape(count * rows, 128) for j in (a, b)], axis=1)
            res = jnp.dot(lhs, w_ref[index - 2], preferred_element_type=F32)
            for p in range(count):
                for c, (j, out) in enumerate(((a, out_a), (b, out_b))):
                    out[p] = finish(res, p, c, (j * count + p) * 8 + index)

    for place, quarter in enumerate(quarters):
        for j, f_ref in enumerate((f0, f1, f2, f3)):
            for i in range(count):
                fac = f_ref[in_quarter(i, spare, quarter)].astype(F32)
                turned = roll64(fac)
                at = pl.ds((j * count + i) * 8, 8)
                fa[at, :] = jnp.where(low, fac, turned)
                fb[at, :] = jnp.where(low, -turned, fac)

        def read_arrived(j, i):
            n = in_quarter(i, spare, quarter)
            first = (((j >> 1) ^ y) * 2 + ((j & 1) ^ core)) * share
            return g_ref[(n >> st) * (4 * share) + first + (n & (share - 1))]

        level(2, inner, read_arrived, x)
        level(3, outer, held(x), x2)
        level(4, bits_ref[2], held(x2), x)
        level(5, bits_ref[3], held(x), x2)
        rest = [x.at[pl.ds(j * count, count)] for j in range(4)]
        done = [o.at[pl.ds(place * count, count)] for o in (o0, o1, o2, o3)]
        across(6, x2, ((0, 1), (2, 3)), ((rest[0], rest[1]), (rest[2], rest[3])))
        across(7, x, ((0, 2), (1, 3)), ((done[0], done[2]), (done[1], done[3])))


def receive(dims, quarters, me_ref, bits_ref, inverse_ref, ri_ref, pieces, out32, stack, t32):
    n_hi, n_lo, share, blocks, rhs = dims
    part_rows = rhs // 4
    y, z1 = me_ref[0], me_ref[2]
    spare, _, _ = spare_bits(bits_ref, dims)
    count = blocks // 4
    lows = lanes_low((part_rows, 128))

    for place, quarter in enumerate(quarters):

        def body(step, carry):
            for part in range(STACKS):
                i = step * STACKS + part
                n = in_quarter(i, spare, quarter)
                for j, p_ref in enumerate(pieces):
                    group = ((j >> 1) ^ y) * 2 + ((j & 1) ^ z1)
                    at = pl.multiple_of(group * part_rows, part_rows)
                    piece = p_ref[place * count + i].astype(F32)
                    stack[part, pl.ds(at, part_rows), :] = jnp.where(lows, piece, -piece).astype(BF16)
                    stack[part, pl.ds(at + rhs, part_rows), :] = roll64(piece).astype(BF16)
                first = pl.multiple_of(n * LEAF, LEAF)
                t32[part * LEAF : (part + 1) * LEAF, :] = lax.dot_general(
                    ri_ref[pl.ds(first, LEAF), :],
                    stack[part],
                    (((1,), (1,)), ((), ())),
                    preferred_element_type=F32,
                )
                for r in range(LEAF):
                    out32[pl.ds(inverse_ref[first + r], 1), :] = t32[part * LEAF + r : part * LEAF + r + 1, :]
            return carry

        lax.fori_loop(0, count // STACKS, body, 0)


def first_receivers(dims, me_ref, bits_ref, inverse_ref, ri_ref, *refs):
    pieces, (out_ref, stack, t32) = refs[:-3], refs[-3:]
    for at, quarters in enumerate(QUARTERS[:-1]):
        receive(
            dims, quarters, me_ref, bits_ref, inverse_ref, ri_ref, pieces[4 * at : 4 * at + 4], out_ref, stack, t32
        )


def last_receivers(dims, me_ref, bits_ref, inverse_ref, ri_ref, p0, p1, p2, p3, done_ref, out_hbm, whole, narrow, sems, stack, t32):
    points = dims[3] * LEAF
    part = points // 4

    def take(step, carry):
        rows = pl.ds(pl.multiple_of(step * 512, 512), 512)
        whole[rows, :] = done_ref[rows, :]
        return carry

    lax.fori_loop(0, points // 512, take, 0)
    receive(dims, QUARTERS[-1], me_ref, bits_ref, inverse_ref, ri_ref, (p0, p1, p2, p3), whole, stack, t32)
    copies = []
    for i in range(4):

        def round_off(step, carry):
            rows = pl.ds(pl.multiple_of(step * 512, 512), 512)
            narrow[rows, :] = whole[rows, :].astype(BF16)
            return carry

        lax.fori_loop(i * (part // 512), (i + 1) * (part // 512), round_off, 0)
        rows = pl.ds(i * part, part)
        copies.append(pltpu.make_async_copy(narrow.at[rows], out_hbm.at[rows], sems.at[i]))
        copies[-1].start()
    for copy in copies:
        copy.wait()


def on_vmem():
    return pl.BlockSpec(memory_space=pltpu.VMEM)


def on_any():
    return pl.BlockSpec(memory_space=pl.ANY)


def on_smem():
    return pl.BlockSpec(memory_space=pltpu.SMEM)


def params(mebibytes):
    return pltpu.CompilerParams(vmem_limit_bytes=mebibytes * 2**20)


def per_device(
    n_hi, n_lo, charges, source_order, source_interp, factors, transfers, level_bits, receiver_interp, receiver_slot
):
    points, twice_rhs = charges.shape
    rhs = twice_rhs // 2
    blocks = points // LEAF
    devices = n_hi * n_lo
    share = blocks // devices
    quarter = rhs // 4
    dims = (n_hi, n_lo, share, blocks, rhs)
    half_hi, half_lo = n_hi // 2 * n_lo, n_lo // 2
    hi, lo = lax.axis_index("hi"), lax.axis_index("lo")
    me = jnp.stack([hi >> (log2(n_hi) - 1), lo & 1, lo >> (log2(n_lo) - 1), hi, lo]).astype(jnp.int32)

    def swapped(device, j):
        flipped = device ^ (half_hi if j >> 1 else 0)
        core, top = flipped & 1, (flipped // half_lo) & 1
        base = flipped - core - top * half_lo
        return base + (core ^ (j & 1)) * half_lo + top

    spread = factors.reshape(n_hi, 2, n_lo // 4, 2, share, 8, 128).transpose(0, 3, 2, 1, 4, 5, 6)
    spread = lax.all_to_all(spread.reshape(blocks, 8, 128), AXES, split_axis=0, concat_axis=0, tiled=True)
    facs = [spread]
    for j in range(1, 4):
        mask = (half_hi if j >> 1 else 0) ^ (j & 1)
        facs.append(lax.ppermute(spread, AXES, [(s, s ^ mask) for s in range(devices)]))

    sent = pl.pallas_call(
        functools.partial(source_kernel, dims),
        out_shape=jax.ShapeDtypeStruct((devices * 4 * share, quarter, 128), BF16),
        in_specs=[on_any(), on_smem()] + [on_any()] * 4,
        out_specs=on_vmem(),
        scratch_shapes=[
            pltpu.SMEM((points,), jnp.int32),
            pltpu.VMEM((points, 128), BF16),
            pltpu.VMEM((points, 128), BF16),
            pltpu.VMEM((blocks * 8, 128), BF16),
            pltpu.VMEM((2,) + transfers.shape[1:], BF16),
            pltpu.SemaphoreType.DMA((8,)),
            pltpu.VMEM((points, 128), F32),
            pltpu.VMEM((blocks, rhs, 128), BF16),
            pltpu.VMEM((blocks * 8, 128), F32),
            pltpu.VMEM((blocks * 8, 128), F32),
            pltpu.VMEM((2, 256, 512), BF16),
        ],
        compiler_params=params(60),
        name="source_side",
    )(source_order, level_bits, charges, source_interp, factors.reshape(blocks * 8, 128), transfers)

    arrived = lax.all_to_all(sent, AXES, split_axis=0, concat_axis=0, tiled=True)

    inverse = pl.pallas_call(
        functools.partial(inverse_kernel, dims),
        out_shape=jax.ShapeDtypeStruct((points,), jnp.int32),
        in_specs=[on_smem(), on_any()],
        out_specs=on_smem(),
        compiler_params=params(12),
        cost_estimate=pl.CostEstimate(flops=10**10, bytes_accessed=2**25, transcendentals=0),
        name="inverse_slots",
    )(receiver_slot, facs[3])

    homes = []
    after = inverse
    for quarters in QUARTERS:
        count = len(quarters) * blocks // 4
        pieces = pl.pallas_call(
            functools.partial(middle_kernel, dims, quarters),
            out_shape=[jax.ShapeDtypeStruct((count, quarter, 128), BF16)] * 4,
            in_specs=[on_smem(), on_smem()] + [on_vmem()] * 6 + [on_any()],
            out_specs=[on_vmem()] * 4,
            scratch_shapes=[
                pltpu.VMEM((blocks, quarter, 128), BF16),
                pltpu.VMEM((blocks, quarter, 128), BF16),
                pltpu.VMEM((blocks * 8, 128), F32),
                pltpu.VMEM((blocks * 8, 128), F32),
                pltpu.VMEM((6, 256, 512), BF16),
            ],
            compiler_params=params(16),
            name="middle_levels",
        )(me, level_bits, arrived, *facs, transfers, after)
        after = pieces[0]
        homes.append(
            [lax.ppermute(pieces[j], AXES, [(s, swapped(s, j)) for s in range(devices)]) for j in range(4)]
        )

    work = [pltpu.VMEM((STACKS, 2 * rhs, 128), BF16), pltpu.VMEM((STACKS * LEAF, 128), F32)]
    done = pl.pallas_call(
        functools.partial(first_receivers, dims),
        out_shape=jax.ShapeDtypeStruct((points, twice_rhs), F32),
        in_specs=[on_smem(), on_smem(), on_smem()] + [on_vmem()] * (4 * len(QUARTERS) - 3),
        out_specs=on_vmem(),
        scratch_shapes=work,
        compiler_params=params(16),
        name="first_receivers",
    )(me, level_bits, inverse, receiver_interp, *[piece for home in homes[:-1] for piece in home])
    return pl.pallas_call(
        functools.partial(last_receivers, dims),
        out_shape=jax.ShapeDtypeStruct((points, twice_rhs), BF16),
        in_specs=[on_smem(), on_smem(), on_smem()] + [on_vmem()] * 6,
        out_specs=on_any(),
        scratch_shapes=[
            pltpu.VMEM((points, 128), F32),
            pltpu.VMEM((points, 128), BF16),
            pltpu.SemaphoreType.DMA((4,)),
        ]
        + work,
        compiler_params=params(24),
        name="last_receivers",
    )(me, level_bits, inverse, receiver_interp, *homes[-1], done)


def solution(mesh):
    body = functools.partial(per_device, mesh.shape["hi"], mesh.shape["lo"])
    return jax.shard_map(
        body,
        mesh=mesh,
        in_specs=(
            P(AXES, None),
            P(AXES),
            P(AXES, None),
            P(AXES, None, None),
            P(),
            P(),
            P(AXES, None),
            P(AXES),
        ),
        out_specs=P(AXES, None),
        check_vma=False,
    )
```

```python
import functools

import jax
import jax.numpy as jnp
from jax import lax
from jax.experimental import pallas as pl
from jax.experimental.pallas import tpu as pltpu
from jax.sharding import PartitionSpec as P

LEAF = 64
AXES = ("hi", "lo")
SPLIT = 16
STACKS = 16
QUARTERS = ((0,), (1,), (2,), (3,))
LEAVES = 32
SPAIRS = 32
F32 = jnp.float32
BF16 = jnp.bfloat16


def log2(value):
    return value.bit_length() - 1


def lanes_low(shape):
    return lax.broadcasted_iota(jnp.int32, shape, len(shape) - 1) < 64


def roll64(value):
    return pltpu.roll(value, 64, 1)


def build_weights(w_ref, slot, tr_ref, level, flip=0):
    for i in range(2):
        for c in range(2):
            piece = tr_ref[level, c ^ flip, i ^ flip].astype(F32)
            turned = roll64(piece)
            turned = jnp.where(lanes_low(piece.shape), -turned, turned)
            block = jnp.concatenate([piece, turned], axis=0).astype(BF16)
            w_ref[slot, i * 128 : (i + 1) * 128, c * 128 : (c + 1) * 128] = block
            across = roll64(jnp.concatenate([piece, turned], axis=0)).astype(BF16)
            w_ref[slot, i * 128 : (i + 1) * 128, 256 + c * 128 : 256 + (c + 1) * 128] = across


def split_factors(read16, fa_ref, fb_ref, first, rows):
    def body(step, carry):
        for part in range(SPLIT):
            at = pl.multiple_of(step * (16 * SPLIT) + part * 16, 16)
            fac = read16(at).astype(F32)
            turned = roll64(fac)
            low = lanes_low(fac.shape)
            fa_ref[pl.ds(first + at, 16), :] = jnp.where(low, fac, turned)
            fb_ref[pl.ds(first + at, 16), :] = jnp.where(low, -turned, fac)
        return carry

    lax.fori_loop(0, rows // (16 * SPLIT), body, 0)


def scaled(value, other, fa_ref, fb_ref, row):
    fa = fa_ref[pl.ds(row, 1), :]
    fb = fb_ref[pl.ds(row, 1), :]
    return (value * fa + other * fb).astype(BF16)


def gather16(rows_ref, index_ref, first):
    iota = lax.broadcasted_iota(jnp.int32, (8, 128), 0)
    halves = []
    for half in range(2):
        acc = None
        for i in range(8):
            at = index_ref[first + half * 8 + i]
            row = jnp.broadcast_to(rows_ref[pl.ds(at, 1), :], (8, 128))
            acc = row if acc is None else jnp.where(iota == i, row, acc)
        halves.append(acc)
    return jnp.concatenate(halves, axis=0).astype(BF16)


def pair_of(k, bit):
    low = k & (lax.shift_left(1, bit) - 1)
    first = lax.shift_left(lax.shift_right_logical(k, bit), bit + 1) | low
    return first, first + lax.shift_left(1, bit)


def source_kernel(
    dims, order_hbm, bits_ref, ch_hbm, si_hbm, fac_hbm, tr_hbm, out_ref,
    order_ref, ch_ref, si_ref, fac_ref, tr_ref, sems, x32, mid_ref, fa, fb, w_ref,
):
    n_hi, n_lo, share, blocks, rhs = dims
    quarter = rhs // 4
    points = blocks * LEAF
    part = points // 4
    copies = [
        pltpu.make_async_copy(ch_hbm.at[pl.ds(i * part, part)], ch_ref.at[pl.ds(i * part, part)], sems.at[i])
        for i in range(4)
    ]
    copies.append(pltpu.make_async_copy(fac_hbm, fac_ref, sems.at[4]))
    copies.append(pltpu.make_async_copy(tr_hbm.at[pl.ds(0, 2)], tr_ref, sems.at[5]))
    copies.append(pltpu.make_async_copy(si_hbm, si_ref, sems.at[6]))
    copies.append(pltpu.make_async_copy(order_hbm, order_ref, sems.at[7]))
    for copy in copies[4:6] + copies[:4] + copies[6:]:
        copy.start()
    copies[5].wait()
    build_weights(w_ref, 0, tr_ref, 0)
    build_weights(w_ref, 1, tr_ref, 1)
    copies[4].wait()
    split_factors(lambda at: fac_ref[pl.ds(at, 16), :], fa, fb, 0, blocks * 8)

    def widen(step, carry):
        rows = pl.ds(pl.multiple_of(step * 512, 512), 512)
        x32[rows, :] = ch_ref[rows, :].astype(F32)
        return carry

    for i in range(4):
        copies[i].wait()
        lax.fori_loop(i * (part // 512), (i + 1) * (part // 512), widen, 0)
    copies[6].wait()
    copies[7].wait()

    def leaf(b):
        first = pl.multiple_of(b * LEAF, LEAF)
        rows = jnp.concatenate([gather16(x32, order_ref, first + g * 16) for g in range(LEAF // 16)], axis=0)
        product = lax.dot_general(
            rows, si_ref[pl.ds(first, LEAF), :], (((0,), (0,)), ((), ())), preferred_element_type=F32
        )
        lower = roll64(product[rhs:])
        lower = jnp.where(lanes_low(lower.shape), -lower, lower)
        return (product[:rhs] + lower).astype(BF16)

    def level(index, pairs, read, store):
        bit = bits_ref[index]

        def body(step, carry):
            ends = [pair_of(step * pairs + p, bit) for p in range(pairs)]
            lhs = jnp.concatenate([jnp.concatenate([read(a), read(b)], axis=1) for a, b in ends], axis=0)
            res = jnp.dot(lhs, w_ref[index], preferred_element_type=F32)
            for p in range(pairs):
                for c in range(2):
                    n = ends[p][c]
                    value = res[p * rhs : (p + 1) * rhs, c * 128 : (c + 1) * 128]
                    other = res[p * rhs : (p + 1) * rhs, 256 + c * 128 : 256 + (c + 1) * 128]
                    store(n, scaled(value, other, fa, fb, n * 8 + index))
            return carry

        lax.fori_loop(0, blocks // 2 // pairs, body, 0)

    st, lm, hh = log2(share), log2(n_lo // 4), log2(n_hi // 2)

    def store_first(n, value):
        mid_ref[n] = value

    def store_second(n, value):
        t = n & (share - 1)
        core = (n >> st) & 1
        lmid = (n >> (st + 1)) & (n_lo // 4 - 1)
        z1 = (n >> (st + 1 + lm)) & 1
        rest = (n >> (st + 2 + lm)) & (n_hi // 2 - 1)
        y = n >> (st + 2 + lm + hh)
        target = rest * n_lo + core * (n_lo // 2) + lmid * 2
        m = (y * 2 + z1) * share + t
        for r in range(4):
            d = target + (r // 2) * (n_hi // 2) * n_lo + r % 2
            out_ref[d * (4 * share) + m] = value[r * quarter : (r + 1) * quarter]

    level(0, LEAVES // 2, leaf, store_first)
    level(1, SPAIRS, lambda n: mid_ref[n], store_second)


def spare_bits(bits_ref, dims):
    n_hi, n_lo, share, blocks, rhs = dims
    inner = log2(share) + log2(n_lo) - 1
    outer = log2(share) + log2(n_lo) + log2(n_hi) - 1
    free = [bit for bit in range(outer) if bit != inner]

    def first_free(after):
        found = jnp.int32(free[-1])
        for bit in reversed(free[:-1]):
            usable = (bits_ref[2] != bit) & (bits_ref[3] != bit) & (bit > after)
            found = jnp.where(usable, bit, found)
        return found

    first = first_free(-1)
    return (first, first_free(first)), inner, outer


def with_bit(i, bit, value):
    low = i & (lax.shift_left(1, bit) - 1)
    return lax.shift_left(lax.shift_right_logical(i, bit), bit + 1) | low | (value << bit)


def in_quarter(i, spare, quarter):
    return with_bit(with_bit(i, spare[0], quarter & 1), spare[1], quarter >> 1)


def inverse_kernel(dims, slot_ref, after_ref, inverse_ref):
    def invert(step, carry):
        for part in range(32):
            at = step * 32 + part
            inverse_ref[slot_ref[at]] = at
        return carry

    lax.fori_loop(0, dims[3] * LEAF // 32, invert, 0)


def middle_kernel(
    dims, quarters, me_ref, bits_ref, g_ref, f0, f1, f2, f3, tr_ref, after_ref, o0, o1, o2, o3, x, x2, fa, fb, w_ref
):
    n_hi, n_lo, share, blocks, rhs = dims
    rows = rhs // 4
    st = log2(share)
    y, core = me_ref[0], me_ref[1]
    spare, inner, outer = spare_bits(bits_ref, dims)
    count = blocks // 4
    low = lanes_low((8, 128))
    for index in range(4):
        build_weights(w_ref, index, tr_ref, index + 2)
    build_weights(w_ref, 4, tr_ref, 6, core)
    build_weights(w_ref, 5, tr_ref, 7, y)

    def finish(res, p, c, row):
        value = res[p * rows : (p + 1) * rows, c * 128 : (c + 1) * 128]
        other = res[p * rows : (p + 1) * rows, 256 + c * 128 : 256 + (c + 1) * 128]
        return scaled(value, other, fa, fb, row)

    def held(x):
        def read(j, i):
            return x[j * count + i]

        return read

    def level(index, bit, read, x):
        packed = bit - (bit > spare[0]).astype(jnp.int32) - (bit > spare[1]).astype(jnp.int32)
        ends = [pair_of(k, packed) for k in range(count // 2)]
        for j in range(4):
            lhs = jnp.concatenate([jnp.concatenate([read(j, a), read(j, b)], axis=1) for a, b in ends], axis=0)
            res = jnp.dot(lhs, w_ref[index - 2], preferred_element_type=F32)
            for p in range(count // 2):
                for c in range(2):
                    n = j * count + ends[p][c]
                    x[n] = finish(res, p, c, n * 8 + index)

    def across(index, x, pairs, outs):
        for (a, b), (out_a, out_b) in zip(pairs, outs):
            lhs = jnp.concatenate([x[pl.ds(j * count, count)].reshape(count * rows, 128) for j in (a, b)], axis=1)
            res = jnp.dot(lhs, w_ref[index - 2], preferred_element_type=F32)
            for p in range(count):
                for c, (j, out) in enumerate(((a, out_a), (b, out_b))):
                    out[p] = finish(res, p, c, (j * count + p) * 8 + index)

    for place, quarter in enumerate(quarters):
        for j, f_ref in enumerate((f0, f1, f2, f3)):
            for i in range(count):
                fac = f_ref[in_quarter(i, spare, quarter)].astype(F32)
                turned = roll64(fac)
                at = pl.ds((j * count + i) * 8, 8)
                fa[at, :] = jnp.where(low, fac, turned)
                fb[at, :] = jnp.where(low, -turned, fac)

        def read_arrived(j, i):
            n = in_quarter(i, spare, quarter)
            first = (((j >> 1) ^ y) * 2 + ((j & 1) ^ core)) * share
            return g_ref[(n >> st) * (4 * share) + first + (n & (share - 1))]

        level(2, inner, read_arrived, x)
        level(3, outer, held(x), x2)
        level(4, bits_ref[2], held(x2), x)
        level(5, bits_ref[3], held(x), x2)
        rest = [x.at[pl.ds(j * count, count)] for j in range(4)]
        done = [o.at[pl.ds(place * count, count)] for o in (o0, o1, o2, o3)]
        across(6, x2, ((0, 1), (2, 3)), ((rest[0], rest[1]), (rest[2], rest[3])))
        across(7, x, ((0, 2), (1, 3)), ((done[0], done[2]), (done[1], done[3])))


def receive(dims, quarters, me_ref, bits_ref, inverse_ref, ri_ref, pieces, out32, stack, t32):
    n_hi, n_lo, share, blocks, rhs = dims
    part_rows = rhs // 4
    y, z1 = me_ref[0], me_ref[2]
    spare, _, _ = spare_bits(bits_ref, dims)
    count = blocks // 4
    lows = lanes_low((part_rows, 128))

    for place, quarter in enumerate(quarters):

        def body(step, carry):
            for part in range(STACKS):
                i = step * STACKS + part
                n = in_quarter(i, spare, quarter)
                for j, p_ref in enumerate(pieces):
                    group = ((j >> 1) ^ y) * 2 + ((j & 1) ^ z1)
                    at = pl.multiple_of(group * part_rows, part_rows)
                    piece = p_ref[place * count + i].astype(F32)
                    stack[part, pl.ds(at, part_rows), :] = jnp.where(lows, piece, -piece).astype(BF16)
                    stack[part, pl.ds(at + rhs, part_rows), :] = roll64(piece).astype(BF16)
                first = pl.multiple_of(n * LEAF, LEAF)
                t32[part * LEAF : (part + 1) * LEAF, :] = lax.dot_general(
                    ri_ref[pl.ds(first, LEAF), :],
                    stack[part],
                    (((1,), (1,)), ((), ())),
                    preferred_element_type=F32,
                )
                for r in range(LEAF):
                    out32[pl.ds(inverse_ref[first + r], 1), :] = t32[part * LEAF + r : part * LEAF + r + 1, :]
            return carry

        lax.fori_loop(0, count // STACKS, body, 0)


def first_receivers(dims, me_ref, bits_ref, inverse_ref, ri_ref, *refs):
    pieces, (out_ref, stack, t32) = refs[:-3], refs[-3:]
    for at, quarters in enumerate(QUARTERS[:-2]):
        receive(
            dims, quarters, me_ref, bits_ref, inverse_ref, ri_ref, pieces[4 * at : 4 * at + 4], out_ref, stack, t32
        )


def last_receivers(dims, me_ref, bits_ref, inverse_ref, ri_ref, *refs):
    early, late, (done_ref, out_hbm, whole, narrow, sems, stack, t32) = refs[:4], refs[4:8], refs[8:]
    points = dims[3] * LEAF
    part = points // 4

    def take(step, carry):
        rows = pl.ds(pl.multiple_of(step * 512, 512), 512)
        whole[rows, :] = done_ref[rows, :]
        return carry

    lax.fori_loop(0, points // 512, take, 0)
    receive(dims, QUARTERS[-2], me_ref, bits_ref, inverse_ref, ri_ref, early, whole, stack, t32)
    receive(dims, QUARTERS[-1], me_ref, bits_ref, inverse_ref, ri_ref, late, whole, stack, t32)
    copies = []
    for i in range(4):

        def round_off(step, carry):
            rows = pl.ds(pl.multiple_of(step * 512, 512), 512)
            narrow[rows, :] = whole[rows, :].astype(BF16)
            return carry

        lax.fori_loop(i * (part // 512), (i + 1) * (part // 512), round_off, 0)
        rows = pl.ds(i * part, part)
        copies.append(pltpu.make_async_copy(narrow.at[rows], out_hbm.at[rows], sems.at[i]))
        copies[-1].start()
    for copy in copies:
        copy.wait()


def on_vmem():
    return pl.BlockSpec(memory_space=pltpu.VMEM)


def on_any():
    return pl.BlockSpec(memory_space=pl.ANY)


def on_smem():
    return pl.BlockSpec(memory_space=pltpu.SMEM)


def params(mebibytes):
    return pltpu.CompilerParams(vmem_limit_bytes=mebibytes * 2**20)


def per_device(
    n_hi, n_lo, charges, source_order, source_interp, factors, transfers, level_bits, receiver_interp, receiver_slot
):
    points, twice_rhs = charges.shape
    rhs = twice_rhs // 2
    blocks = points // LEAF
    devices = n_hi * n_lo
    share = blocks // devices
    quarter = rhs // 4
    dims = (n_hi, n_lo, share, blocks, rhs)
    half_hi, half_lo = n_hi // 2 * n_lo, n_lo // 2
    hi, lo = lax.axis_index("hi"), lax.axis_index("lo")
    me = jnp.stack([hi >> (log2(n_hi) - 1), lo & 1, lo >> (log2(n_lo) - 1), hi, lo]).astype(jnp.int32)

    def swapped(device, j):
        flipped = device ^ (half_hi if j >> 1 else 0)
        core, top = flipped & 1, (flipped // half_lo) & 1
        base = flipped - core - top * half_lo
        return base + (core ^ (j & 1)) * half_lo + top

    spread = factors.reshape(n_hi, 2, n_lo // 4, 2, share, 8, 128).transpose(0, 3, 2, 1, 4, 5, 6)
    spread = lax.all_to_all(spread.reshape(blocks, 8, 128), AXES, split_axis=0, concat_axis=0, tiled=True)
    facs = [spread]
    for j in range(1, 4):
        mask = (half_hi if j >> 1 else 0) ^ (j & 1)
        facs.append(lax.ppermute(spread, AXES, [(s, s ^ mask) for s in range(devices)]))

    sent = pl.pallas_call(
        functools.partial(source_kernel, dims),
        out_shape=jax.ShapeDtypeStruct((devices * 4 * share, quarter, 128), BF16),
        in_specs=[on_any(), on_smem()] + [on_any()] * 4,
        out_specs=on_vmem(),
        scratch_shapes=[
            pltpu.SMEM((points,), jnp.int32),
            pltpu.VMEM((points, 128), BF16),
            pltpu.VMEM((points, 128), BF16),
            pltpu.VMEM((blocks * 8, 128), BF16),
            pltpu.VMEM((2,) + transfers.shape[1:], BF16),
            pltpu.SemaphoreType.DMA((8,)),
            pltpu.VMEM((points, 128), F32),
            pltpu.VMEM((blocks, rhs, 128), BF16),
            pltpu.VMEM((blocks * 8, 128), F32),
            pltpu.VMEM((blocks * 8, 128), F32),
            pltpu.VMEM((2, 256, 512), BF16),
        ],
        compiler_params=params(60),
        name="source_side",
    )(source_order, level_bits, charges, source_interp, factors.reshape(blocks * 8, 128), transfers)

    arrived = lax.all_to_all(sent, AXES, split_axis=0, concat_axis=0, tiled=True)

    inverse = pl.pallas_call(
        functools.partial(inverse_kernel, dims),
        out_shape=jax.ShapeDtypeStruct((points,), jnp.int32),
        in_specs=[on_smem(), on_any()],
        out_specs=on_smem(),
        compiler_params=params(12),
        cost_estimate=pl.CostEstimate(flops=10**10, bytes_accessed=2**25, transcendentals=0),
        name="inverse_slots",
    )(receiver_slot, facs[3])

    homes = []
    after = inverse
    for quarters in QUARTERS:
        count = len(quarters) * blocks // 4
        pieces = pl.pallas_call(
            functools.partial(middle_kernel, dims, quarters),
            out_shape=[jax.ShapeDtypeStruct((count, quarter, 128), BF16)] * 4,
            in_specs=[on_smem(), on_smem()] + [on_vmem()] * 6 + [on_any()],
            out_specs=[on_vmem()] * 4,
            scratch_shapes=[
                pltpu.VMEM((blocks, quarter, 128), BF16),
                pltpu.VMEM((blocks, quarter, 128), BF16),
                pltpu.VMEM((blocks * 8, 128), F32),
                pltpu.VMEM((blocks * 8, 128), F32),
                pltpu.VMEM((6, 256, 512), BF16),
            ],
            compiler_params=params(16),
            name="middle_levels",
        )(me, level_bits, arrived, *facs, transfers, after)
        after = pieces[0]
        homes.append(
            [lax.ppermute(pieces[j], AXES, [(s, swapped(s, j)) for s in range(devices)]) for j in range(4)]
        )

    work = [pltpu.VMEM((STACKS, 2 * rhs, 128), BF16), pltpu.VMEM((STACKS * LEAF, 128), F32)]
    done = pl.pallas_call(
        functools.partial(first_receivers, dims),
        out_shape=jax.ShapeDtypeStruct((points, twice_rhs), F32),
        in_specs=[on_smem(), on_smem(), on_smem()] + [on_vmem()] * (4 * len(QUARTERS) - 7),
        out_specs=on_vmem(),
        scratch_shapes=work,
        compiler_params=params(16),
        name="first_receivers",
    )(me, level_bits, inverse, receiver_interp, *[piece for home in homes[:-2] for piece in home])
    return pl.pallas_call(
        functools.partial(last_receivers, dims),
        out_shape=jax.ShapeDtypeStruct((points, twice_rhs), BF16),
        in_specs=[on_smem(), on_smem(), on_smem()] + [on_vmem()] * 10,
        out_specs=on_any(),
        scratch_shapes=[
            pltpu.VMEM((points, 128), F32),
            pltpu.VMEM((points, 128), BF16),
            pltpu.SemaphoreType.DMA((4,)),
        ]
        + work,
        compiler_params=params(24),
        name="last_receivers",
    )(me, level_bits, inverse, receiver_interp, *homes[-2], *homes[-1], done)


def solution(mesh):
    body = functools.partial(per_device, mesh.shape["hi"], mesh.shape["lo"])
    return jax.shard_map(
        body,
        mesh=mesh,
        in_specs=(
            P(AXES, None),
            P(AXES),
            P(AXES, None),
            P(AXES, None, None),
            P(),
            P(),
            P(AXES, None),
            P(AXES),
        ),
        out_specs=P(AXES, None),
        check_vma=False,
    )
```
